32 devices in a mesh: grp: 2 (over y), blk: 8 (over z, core), tm: 2 (over x), rep: 1.
Axes of the slice: x: 2, y: 2, z: 4, core: 2. Of those that a mesh axis runs over, the one named last changes fastest.
Arguments:
- factor_rows: bfloat16 [8192, 2048], P(('grp', 'blk')), parts along dimension 0, may hold values from -0.125 to 0.125
- noise: bfloat16 [8192, 8192], P(('grp', 'blk'), ('tm', 'rep')), parts along dimension 0, may hold values from -6 to 6
- time_kernel: float32 [8192], replicated, may hold values from -0.0625 to 0.0625
- region_of_block: int32 [16], P('grp'), parts along dimension 0, may hold values from 0 to 3, as said below
Outputs:
- field: bfloat16 [8192, 8192], P(('grp', 'blk', 'tm', 'rep')), parts along dimension 0
The draws below stay inside these ranges and needn't reach their ends.
There are 2 independent parts, one for each index of `grp`. The reference program is written for one: setup_inputs(seed, part) draws one part's arguments, and reference() takes and returns one part's arrays. A program takes and returns all parts, laid end to end along the dimension named above; an argument that names none is the same for every part. Nothing has to cross between parts.
Inputs may be any that keep to these rules, and one draw needn't show every extreme that they name: `region_of_block`: each part is its own table: within one part, the blocks of one region are consecutive, region numbers never fall from block to block and every region from 0 to 3 appears; a region holds 1 to 4 blocks, and some region holds exactly 4. The next part starts again at region 0.
All inputs are finite; a program needn't handle non-finite values.
Results may differ from the reference program's by a relative error of at most 0.0049.
Values may be sent and summed in bfloat16 or wider, within the bound.
A program may use at most 128 MiB of HBM per device.

```python
import jax
import jax.numpy as jnp
from jax import lax

BLOCK = 512
MAXC = 4
DAYS = 8192
BLOCKS = 8
STATIONS = 4096
REGIONS = 4


def draw_region_of_block(key, part):
    order = jax.random.permutation(jax.random.fold_in(key, 7), REGIONS)
    rank = jnp.argsort(order).astype(jnp.int32)
    lengths = jnp.where(rank == 0, MAXC, jnp.where(rank <= MAXC - 2, 1, 2)).astype(jnp.int32)
    ends = jnp.cumsum(lengths).astype(jnp.int32)
    block_ids = jnp.arange(BLOCKS, dtype=jnp.int32)
    return jnp.sum((ends[None, :] <= block_ids[:, None]).astype(jnp.int32), axis=1).astype(jnp.int32)


def block_scale(own_key, extent, shards, least, top_value):
    def one(dim, parts):
        draws = jax.random.uniform(jax.random.fold_in(jax.random.fold_in(own_key, 6), dim), (parts,), jnp.float32, least / len(shards), top_value / len(shards))
        return jnp.repeat(jnp.exp(draws), extent[dim] // parts).reshape((-1,) + (1,) * (len(extent) - dim - 1))

    level = one(*shards[0])
    for cut in shards[1:]:
        level = level * one(*cut)
    return level


def scatter_about(stream_key, extent, deviation, reach, pieces=(), held_as=jnp.bfloat16):
    loudness = block_scale(stream_key, extent, pieces, -0.22, 0.18) if pieces else 1.0
    values = jax.random.normal(stream_key, extent, jnp.float32) * deviation * loudness
    return jnp.minimum(jnp.maximum(values, -reach), reach).astype(held_as)


def setup_inputs(seed: int = 0, part: int = 0) -> dict:
    keys = jax.random.split(jax.random.key(seed), 5)
    own_keys = jax.random.split(jax.random.fold_in(keys[4], part), 5)
    return {
        "factor_rows": scatter_about(own_keys[0], (STATIONS, MAXC * BLOCK), (MAXC * BLOCK) ** -0.5, 0.125, ((0, 8),)),
        "noise": scatter_about(own_keys[1], (STATIONS, DAYS), 1.0, 6.0, ((0, 8), (1, 2))),
        "time_kernel": scatter_about(keys[2], (DAYS,), DAYS ** -0.5, 0.0625, (), jnp.float32),
        "region_of_block": draw_region_of_block(jax.random.fold_in(jax.random.fold_in(keys[4], part), 71), part),
    }


def reference(factor_rows, noise, time_kernel, region_of_block):
    blocks = noise.shape[0] // BLOCK
    row_ids = lax.broadcasted_iota(jnp.int32, (BLOCK, BLOCK), 0)
    col_ids = lax.broadcasted_iota(jnp.int32, (BLOCK, BLOCK), 1)
    lower = row_ids >= col_ids
    kernel_spectrum = jnp.fft.rfft(time_kernel.astype(jnp.float32))

    def one_block(index):
        rows = lax.dynamic_slice_in_dim(factor_rows, (index * BLOCK).astype(jnp.int32), BLOCK, 0).astype(jnp.float32)
        own = region_of_block[index]
        total = jnp.zeros((BLOCK, DAYS), jnp.float32)
        for step in range(MAXC):
            source = jnp.maximum(index - step, 0).astype(jnp.int32)
            valid = (index >= step) & (region_of_block[source] == own)
            tile = rows[:, step * BLOCK:(step + 1) * BLOCK]
            if step == 0:
                tile = jnp.where(lower, tile, jnp.zeros_like(tile))
            part = lax.dynamic_slice_in_dim(noise, (source * BLOCK).astype(jnp.int32), BLOCK, 0).astype(jnp.float32)
            product = jnp.dot(tile, part, preferred_element_type=jnp.float32, precision=lax.Precision.HIGHEST)
            total = total + jnp.where(valid, product, jnp.zeros_like(product))
        spatial = lax.optimization_barrier(total.astype(jnp.bfloat16)).astype(jnp.float32)
        filtered = jnp.fft.irfft(jnp.fft.rfft(spatial, axis=1) * kernel_spectrum[None, :], n=DAYS, axis=1)
        return filtered.astype(jnp.bfloat16)

    result = lax.map(one_block, jnp.arange(blocks, dtype=jnp.int32))
    return result.reshape(blocks * BLOCK, DAYS)
```

```python
import math

import jax
import jax.numpy as jnp
from jax import lax
from jax.experimental import pallas as pl
from jax.experimental.pallas import tpu as pltpu
from jax.sharding import PartitionSpec as P

FIRST = 64
CHUNK = 512
TILE = 256
AHEAD = 2
MESH = pl.DeviceIdType.MESH


def shifted(block, axis, distance):
    devices = range(lax.axis_size(axis))
    route = [(i - distance, i) for i in devices if i - distance in devices]
    return lax.ppermute(block, axis, route)


def make_tables(first, second):
    total = first * second
    row_a = lax.broadcasted_iota(jnp.int32, (first, first), 0)
    col_a = lax.broadcasted_iota(jnp.int32, (first, first), 1)
    angle_one = 2.0 * math.pi / first * (row_a * col_a % first).astype(jnp.float32)
    row_t = lax.broadcasted_iota(jnp.int32, (first, second), 0)
    col_t = lax.broadcasted_iota(jnp.int32, (first, second), 1)
    angle_tw = 2.0 * math.pi / total * (row_t * col_t % total).astype(jnp.float32)
    row_b = lax.broadcasted_iota(jnp.int32, (second, second), 0)
    col_b = lax.broadcasted_iota(jnp.int32, (second, second), 1)
    angle_two = 2.0 * math.pi / second * (row_b * col_b % second).astype(jnp.float32)
    return (
        jnp.cos(angle_one),
        -jnp.sin(angle_one),
        jnp.cos(angle_tw),
        -jnp.sin(angle_tw),
        jnp.cos(angle_two),
        -jnp.sin(angle_two),
    )


def left_apply(table, values):
    return jnp.einsum(
        "kn,rnm->rkm", table, values.astype(jnp.float32), precision=lax.Precision.HIGH
    )


def right_apply(values, table):
    return jnp.einsum("rkn,nm->rkm", values, table, precision=lax.Precision.HIGH)


def forward(sig_re, sig_im, tables):
    one_re, one_im, tw_re, tw_im, two_re, two_im = tables
    first_re = left_apply(one_re, sig_re) - left_apply(one_im, sig_im)
    first_im = left_apply(one_re, sig_im) + left_apply(one_im, sig_re)
    turned_re = first_re * tw_re - first_im * tw_im
    turned_im = first_re * tw_im + first_im * tw_re
    spec_re = right_apply(turned_re, two_re) - right_apply(turned_im, two_im)
    spec_im = right_apply(turned_re, two_im) + right_apply(turned_im, two_re)
    return (spec_re, spec_im)


def inverse(spec_re, spec_im, tables):
    one_re, one_im, tw_re, tw_im, two_re, two_im = tables
    back_re = right_apply(spec_re, two_re) + right_apply(spec_im, two_im)
    back_im = right_apply(spec_im, two_re) - right_apply(spec_re, two_im)
    turned_re = back_re * tw_re + back_im * tw_im
    turned_im = back_im * tw_re - back_re * tw_im
    total = one_re.shape[0] * two_re.shape[0]
    out_re = (left_apply(one_re, turned_re) + left_apply(one_im, turned_im)) / total
    out_im = (left_apply(one_re, turned_im) - left_apply(one_im, turned_re)) / total
    return (out_re, out_im)


def on_device(factor_rows, noise, time_kernel, region_of_block):
    width = noise.shape[0]
    slots = factor_rows.shape[1] // width
    position = lax.axis_index("blk")
    own_region = lax.dynamic_index_in_dim(region_of_block, position, 0, keepdims=False)
    row_ids = lax.broadcasted_iota(jnp.int32, (width, width), 0)
    col_ids = lax.broadcasted_iota(jnp.int32, (width, width), 1)
    diagonal_tile = jnp.where(
        row_ids >= col_ids, factor_rows[:, :width], jnp.zeros((width, width), jnp.bfloat16)
    )
    total = jnp.dot(diagonal_tile, noise, preferred_element_type=jnp.float32)
    previous = noise
    for step in range(1, slots):
        previous = shifted(noise, "blk", step)
        source = jnp.maximum(position - step, 0)
        source_region = lax.dynamic_index_in_dim(region_of_block, source, 0, keepdims=False)
        valid = (position >= step) & (source_region == own_region)
        tile = factor_rows[:, step * width : (step + 1) * width]
        product = jnp.dot(tile, previous, preferred_element_type=jnp.float32)
        total = total + jnp.where(valid, product, jnp.zeros_like(product))
    spatial = total.astype(jnp.bfloat16)
    regrouped = lax.all_to_all(spatial, ("tm", "rep"), split_axis=0, concat_axis=1, tiled=True)
    days = regrouped.shape[1]
    stations = regrouped.shape[0]
    second = days // FIRST
    tables = make_tables(FIRST, second)
    paired = regrouped.reshape(stations // 2, 2, FIRST, second)
    sig_re = paired[:, 0]
    sig_im = paired[:, 1]
    kernel_sig = time_kernel.reshape(1, FIRST, second)
    kernel_re, kernel_im = forward(kernel_sig, jnp.zeros_like(kernel_sig), tables)
    spec_re, spec_im = forward(sig_re, sig_im, tables)
    prod_re = spec_re * kernel_re - spec_im * kernel_im
    prod_im = spec_re * kernel_im + spec_im * kernel_re
    out_re, out_im = inverse(prod_re, prod_im, tables)
    joined = jnp.stack((out_re, out_im), axis=1)
    return joined.reshape(stations, days).astype(jnp.bfloat16)


def sample_kernel(
    factor, noise, time_kernel, regions, out,
    weights, partial_weights, above, up_in, side_in, sibling, partial,
    kept, given, got, toeplitz, acc,
    up_send, up_recv, side_send, side_recv, sib_send, sib_recv, x_send, x_recv, tile_send, tile_recv,
):
    blocks = lax.axis_size("blk")
    block = lax.axis_index("blk")
    half = lax.axis_index("tm")
    core = lax.rem(block, 2)
    chip = lax.div(block, 2)
    first_chip = chip == 0
    last_chip = chip == blocks // 2 - 1
    sib = block + 1 - 2 * core
    width, local_days = noise.shape
    chunks, _, chunk = up_in.shape
    rows = width // 2
    days = acc.shape[1]

    def cols(step):
        return pl.ds(pl.multiple_of(step * chunk, chunk), chunk)

    def remote(src, dst, send, recv, where):
        return pltpu.make_async_remote_copy(
            src_ref=src, dst_ref=dst, send_sem=send, recv_sem=recv, device_id=where, device_id_type=MESH
        )

    def up_noise(step):
        return remote(noise.at[:, cols(step)], up_in.at[step], up_send.at[step], up_recv.at[step], {"blk": block + 2})

    def up_partial(step):
        return remote(partial.at[step], up_in.at[step], up_send.at[step], up_recv.at[step], {"blk": block + 2})

    def side(step):
        return remote(up_in.at[step], side_in.at[step], side_send.at[step], side_recv.at[step], {"blk": sib})

    def sib_copy(step):
        return remote(noise.at[:, cols(step)], sibling.at[step], sib_send.at[step], sib_recv.at[step], {"blk": sib})

    def cross(step):
        return remote(given.at[step], got.at[step], x_send.at[step], x_recv.at[step], {"tm": 1 - half})

    def tiles_down():
        return remote(factor.at[:, pl.ds(2 * width, 2 * width)], above, tile_send, tile_recv, {"blk": block - 2})

    barrier = pltpu.get_barrier_semaphore()
    pl.semaphore_signal(barrier, inc=1, device_id={"blk": sib}, device_id_type=MESH)
    pl.semaphore_signal(barrier, inc=1, device_id={"tm": 1 - half}, device_id_type=MESH)

    @pl.when(jnp.logical_not(first_chip))
    def _():
        pl.semaphore_signal(barrier, inc=1, device_id={"blk": block - 2}, device_id_type=MESH)

    @pl.when(jnp.logical_not(last_chip))
    def _():
        pl.semaphore_signal(barrier, inc=1, device_id={"blk": block + 2}, device_id_type=MESH)

    pl.semaphore_wait(barrier, 2 + jnp.where(first_chip, 0, 1) + jnp.where(last_chip, 0, 1))

    low = core == 0
    high = core == 1
    sends_up = jnp.logical_not(last_chip)
    takes_up = jnp.logical_not(first_chip)

    @pl.when(low & takes_up)
    def _():
        tiles_down().start()

    @pl.when(high & sends_up)
    def _():
        for step in range(AHEAD):
            up_noise(step).start()

    @pl.when(low)
    def _():
        for step in range(AHEAD):
            sib_copy(step).start()

    def valid(index, back):
        inside = index >= back
        same = regions[jnp.maximum(index - back, 0)] == regions[index]
        return jnp.where(inside & same, 1.0, 0.0).astype(jnp.float32)

    v1, v2, v3 = valid(block, 1), valid(block, 2), valid(block, 3)
    is_low = jnp.where(low, 1.0, 0.0).astype(jnp.float32)
    is_high = 1.0 - is_low
    strip = 64

    def make_weights(index, carry):
        at = pl.ds(pl.multiple_of(index * strip, strip), strip)
        row = lax.broadcasted_iota(jnp.int32, (strip, width), 0) + index * strip
        col = lax.broadcasted_iota(jnp.int32, (strip, width), 1)
        t0, t1, t2, t3 = (factor[at, pl.ds(k * width, width)].astype(jnp.float32) for k in range(4))
        eye = jnp.where(row == col, 1.0, 0.0)
        near = v1 * t1
        mid = v2 * t2
        far = v3 * t3
        first = is_low * (v3 * eye + (1.0 - v3) * mid) + is_high * mid
        second = is_low * near + is_high * far
        weights[at, pl.ds(0, width)] = jnp.where(row >= col, t0, 0.0).astype(jnp.bfloat16)
        weights[at, pl.ds(width, width)] = (is_high * near).astype(jnp.bfloat16)
        weights[at, pl.ds(2 * width, width)] = first.astype(jnp.bfloat16)
        weights[at, pl.ds(3 * width, width)] = second.astype(jnp.bfloat16)
        return carry

    lax.fori_loop(0, width // strip, make_weights, 0)

    line = jnp.broadcast_to(time_kernel[...], (16, days))
    row_of = lax.broadcasted_iota(jnp.int32, (16, days), 0)
    acc[pl.ds(0, 16), :] = line

    def add_row(index, carry):
        acc[pl.ds(0, 16), :] = jnp.where(row_of == index, pltpu.roll(line, index, 1), acc[pl.ds(0, 16), :])
        return carry

    lax.fori_loop(1, 16, add_row, 0)

    def make_toeplitz(index, carry):
        turned = pltpu.roll(acc[pl.ds(0, 16), :], index * 16, 1)
        toeplitz[pl.ds(pl.multiple_of(index * 16, 16), 16), :] = turned.astype(jnp.bfloat16)
        return carry

    lax.fori_loop(0, TILE // 16, make_toeplitz, 0)

    def clear(index, carry):
        acc[:, pl.ds(pl.multiple_of(index * TILE, TILE), TILE)] = jnp.zeros((rows, TILE), jnp.float32)
        return carry

    lax.fori_loop(0, days // TILE, clear, 0)

    @pl.when(low & sends_up)
    def _():
        tiles_down().wait_recv()
        uses = valid(jnp.minimum(block + 2, blocks - 1), 3)

        def make_partial_weights(index, carry):
            at = pl.ds(pl.multiple_of(index * strip, strip), strip)
            row = lax.broadcasted_iota(jnp.int32, (strip, width), 0) + index * strip
            col = lax.broadcasted_iota(jnp.int32, (strip, width), 1)
            t2, t3 = (above[at, pl.ds(k * width, width)].astype(jnp.float32) for k in range(2))
            eye = jnp.where(row == col, 1.0, 0.0)
            partial_weights[at, pl.ds(0, width)] = (uses * t2 + (1.0 - uses) * eye).astype(jnp.bfloat16)
            partial_weights[at, pl.ds(width, width)] = (uses * t3).astype(jnp.bfloat16)
            return carry

        lax.fori_loop(0, width // strip, make_partial_weights, 0)

    def dot(left, right):
        return jnp.dot(left, right, preferred_element_type=jnp.float32)

    def send_stage(step):
        nothing = jnp.zeros((width, chunk), jnp.bfloat16)

        @pl.when(high & sends_up & (step + AHEAD < chunks))
        def _():
            up_noise(step).wait_send()
            up_noise(step + AHEAD).start()

        @pl.when(low & (step + AHEAD < chunks))
        def _():
            sib_copy(step + AHEAD).start()

        @pl.when(high & takes_up)
        def _():
            up_noise(step).wait_recv()
            side(step).start()

        @pl.when(low & takes_up)
        def _():
            side(step).wait_recv()

        @pl.when(first_chip)
        def _():
            side_in[step] = nothing
            up_in[step] = nothing

        @pl.when(low)
        def _():
            sibling[step] = nothing

        @pl.when(low & sends_up)
        def _():
            for part in range(0, width, rows):
                at = pl.ds(part, rows)
                total = dot(partial_weights[at, pl.ds(0, width)], noise[:, cols(step)])
                total += dot(partial_weights[at, pl.ds(width, width)], side_in[step])
                partial[step, at, :] = total.astype(jnp.bfloat16)
            up_partial(step).start()

    def spatial(step, at):
        total = dot(weights[at, pl.ds(0, width)], noise[:, cols(step)])
        total += dot(weights[at, pl.ds(width, width)], sibling[step])
        total += dot(weights[at, pl.ds(2 * width, width)], up_in[step])
        total += dot(weights[at, pl.ds(3 * width, width)], side_in[step])
        return total.astype(jnp.bfloat16)

    def mix_stage(step):
        @pl.when(low & takes_up)
        def _():
            up_partial(step).wait_recv()
            side(step).start()

        @pl.when(high & takes_up)
        def _():
            side(step).wait_recv()

        @pl.when(high)
        def _():
            sib_copy(step).wait_recv()

        given[step] = spatial(step, pl.ds(pl.multiple_of((1 - half) * rows, rows), rows))
        cross(step).start()
        kept[step] = spatial(step, pl.ds(pl.multiple_of(half * rows, rows), rows))

    def filter_stage(step):
        cross(step).wait_recv()
        mine = half * local_days + step * chunk
        other = (1 - half) * local_days + step * chunk

        def one(index, carry):
            at = index * TILE
            parts = []
            for start in (mine, other):
                for piece in range(0, chunk, TILE):
                    offset = lax.rem(at - start - piece + days, days)
                    parts.append(toeplitz[:, pl.ds(pl.multiple_of(offset, TILE), TILE)])
            left = jnp.concatenate([kept[step], got[step]], axis=1)
            right = jnp.concatenate(parts, axis=0)
            acc[:, pl.ds(pl.multiple_of(at, TILE), TILE)] += dot(left, right)
            return carry

        lax.fori_loop(0, days // TILE, one, 0, unroll=4)

    def body(turn, carry):
        @pl.when(turn < chunks)
        def _():
            send_stage(turn)

        @pl.when((turn >= 1) & (turn <= chunks))
        def _():
            mix_stage(turn - 1)

        @pl.when(turn >= 2)
        def _():
            filter_stage(turn - 2)

        return carry

    lax.fori_loop(0, chunks + 2, body, 0)

    def finish(index, carry):
        at = pl.ds(pl.multiple_of(index * TILE, TILE), TILE)
        out[:, at] = acc[:, at].astype(jnp.bfloat16)
        return carry

    lax.fori_loop(0, days // TILE, finish, 0)

    def drain(step, carry):
        cross(step).wait_send()

        @pl.when(takes_up)
        def _():
            side(step).wait_send()

        @pl.when(low)
        def _():
            sib_copy(step).wait_send()

        @pl.when(low & sends_up)
        def _():
            up_partial(step).wait_send()

        @pl.when(high & sends_up & (step + AHEAD >= chunks))
        def _():
            up_noise(step).wait_send()

        return carry

    lax.fori_loop(0, chunks, drain, 0)

    @pl.when(low & takes_up)
    def _():
        tiles_down().wait_send()


def fused(factor_rows, noise, time_kernel, region_of_block):
    width, local_days = noise.shape
    days = time_kernel.shape[0]
    chunks = local_days // CHUNK
    rows = width // 2
    vmem = pl.BlockSpec(memory_space=pltpu.VMEM)
    half = jnp.bfloat16
    pair = [pltpu.SemaphoreType.DMA((chunks,))] * 2
    return pl.pallas_call(
        sample_kernel,
        out_shape=jax.ShapeDtypeStruct((rows, days), half),
        in_specs=[vmem, vmem, vmem, pl.BlockSpec(memory_space=pltpu.SMEM)],
        out_specs=vmem,
        scratch_shapes=[
            pltpu.VMEM((width, 4 * width), half),
            pltpu.VMEM((width, 2 * width), half),
            pltpu.VMEM((width, 2 * width), half),
            pltpu.VMEM((chunks, width, CHUNK), half),
            pltpu.VMEM((chunks, width, CHUNK), half),
            pltpu.VMEM((chunks, width, CHUNK), half),
            pltpu.VMEM((chunks, width, CHUNK), half),
            pltpu.VMEM((chunks, rows, CHUNK), half),
            pltpu.VMEM((chunks, rows, CHUNK), half),
            pltpu.VMEM((chunks, rows, CHUNK), half),
            pltpu.VMEM((TILE, days), half),
            pltpu.VMEM((rows, days), jnp.float32),
        ]
        + pair * 4
        + [pltpu.SemaphoreType.DMA, pltpu.SemaphoreType.DMA],
        compiler_params=pltpu.CompilerParams(
            collective_id=0, has_side_effects=True, vmem_limit_bytes=60 * 1024 * 1024
        ),
        cost_estimate=pl.CostEstimate(
            flops=2 * rows * days * days + 8 * width * width * local_days,
            bytes_accessed=4 * width * local_days + 8 * width * width,
            transcendentals=0,
        ),
    )(factor_rows, noise, time_kernel.reshape(1, days), region_of_block)


def solution(mesh):
    placed = (P(("grp", "blk"), None), P(("grp", "blk"), ("tm", "rep")), P(), P("grp"))
    sizes = dict(mesh.shape)
    paired = sizes["tm"] == 2 and sizes["rep"] == 1 and sizes["blk"] % 2 == 0

    def program(factor_rows, noise, time_kernel, region_of_block):
        width, local_days = noise.shape
        fits = width == 2 * TILE and factor_rows.shape[1] == 4 * width
        fits = fits and local_days % CHUNK == 0 and local_days >= AHEAD * CHUNK
        run = fused if paired and fits else on_device
        return run(factor_rows, noise, time_kernel, region_of_block)

    return jax.shard_map(
        program,
        mesh=mesh,
        in_specs=placed,
        out_specs=P(("grp", "blk", "tm", "rep"), None),
        check_vma=False,
    )
```

```python
import math

import jax
import jax.numpy as jnp
from jax import lax
from jax.experimental import pallas as pl
from jax.experimental.pallas import tpu as pltpu
from jax.sharding import PartitionSpec as P

FIRST = 64
CHUNK = 256
TILE = 256
AHEAD = 6
LEAD = 3
MESH = pl.DeviceIdType.MESH


def shifted(block, axis, distance):
    devices = range(lax.axis_size(axis))
    route = [(i - distance, i) for i in devices if i - distance in devices]
    return lax.ppermute(block, axis, route)


def make_tables(first, second):
    total = first * second
    row_a = lax.broadcasted_iota(jnp.int32, (first, first), 0)
    col_a = lax.broadcasted_iota(jnp.int32, (first, first), 1)
    angle_one = 2.0 * math.pi / first * (row_a * col_a % first).astype(jnp.float32)
    row_t = lax.broadcasted_iota(jnp.int32, (first, second), 0)
    col_t = lax.broadcasted_iota(jnp.int32, (first, second), 1)
    angle_tw = 2.0 * math.pi / total * (row_t * col_t % total).astype(jnp.float32)
    row_b = lax.broadcasted_iota(jnp.int32, (second, second), 0)
    col_b = lax.broadcasted_iota(jnp.int32, (second, second), 1)
    angle_two = 2.0 * math.pi / second * (row_b * col_b % second).astype(jnp.float32)
    return (
        jnp.cos(angle_one),
        -jnp.sin(angle_one),
        jnp.cos(angle_tw),
        -jnp.sin(angle_tw),
        jnp.cos(angle_two),
        -jnp.sin(angle_two),
    )


def left_apply(table, values):
    return jnp.einsum(
        "kn,rnm->rkm", table, values.astype(jnp.float32), precision=lax.Precision.HIGH
    )


def right_apply(values, table):
    return jnp.einsum("rkn,nm->rkm", values, table, precision=lax.Precision.HIGH)


def forward(sig_re, sig_im, tables):
    one_re, one_im, tw_re, tw_im, two_re, two_im = tables
    first_re = left_apply(one_re, sig_re) - left_apply(one_im, sig_im)
    first_im = left_apply(one_re, sig_im) + left_apply(one_im, sig_re)
    turned_re = first_re * tw_re - first_im * tw_im
    turned_im = first_re * tw_im + first_im * tw_re
    spec_re = right_apply(turned_re, two_re) - right_apply(turned_im, two_im)
    spec_im = right_apply(turned_re, two_im) + right_apply(turned_im, two_re)
    return (spec_re, spec_im)


def inverse(spec_re, spec_im, tables):
    one_re, one_im, tw_re, tw_im, two_re, two_im = tables
    back_re = right_apply(spec_re, two_re) + right_apply(spec_im, two_im)
    back_im = right_apply(spec_im, two_re) - right_apply(spec_re, two_im)
    turned_re = back_re * tw_re + back_im * tw_im
    turned_im = back_im * tw_re - back_re * tw_im
    total = one_re.shape[0] * two_re.shape[0]
    out_re = (left_apply(one_re, turned_re) + left_apply(one_im, turned_im)) / total
    out_im = (left_apply(one_re, turned_im) - left_apply(one_im, turned_re)) / total
    return (out_re, out_im)


def on_device(factor_rows, noise, time_kernel, region_of_block):
    width = noise.shape[0]
    slots = factor_rows.shape[1] // width
    position = lax.axis_index("blk")
    own_region = lax.dynamic_index_in_dim(region_of_block, position, 0, keepdims=False)
    row_ids = lax.broadcasted_iota(jnp.int32, (width, width), 0)
    col_ids = lax.broadcasted_iota(jnp.int32, (width, width), 1)
    diagonal_tile = jnp.where(
        row_ids >= col_ids, factor_rows[:, :width], jnp.zeros((width, width), jnp.bfloat16)
    )
    total = jnp.dot(diagonal_tile, noise, preferred_element_type=jnp.float32)
    previous = noise
    for step in range(1, slots):
        previous = shifted(noise, "blk", step)
        source = jnp.maximum(position - step, 0)
        source_region = lax.dynamic_index_in_dim(region_of_block, source, 0, keepdims=False)
        valid = (position >= step) & (source_region == own_region)
        tile = factor_rows[:, step * width : (step + 1) * width]
        product = jnp.dot(tile, previous, preferred_element_type=jnp.float32)
        total = total + jnp.where(valid, product, jnp.zeros_like(product))
    spatial = total.astype(jnp.bfloat16)
    regrouped = lax.all_to_all(spatial, ("tm", "rep"), split_axis=0, concat_axis=1, tiled=True)
    days = regrouped.shape[1]
    stations = regrouped.shape[0]
    second = days // FIRST
    tables = make_tables(FIRST, second)
    paired = regrouped.reshape(stations // 2, 2, FIRST, second)
    sig_re = paired[:, 0]
    sig_im = paired[:, 1]
    kernel_sig = time_kernel.reshape(1, FIRST, second)
    kernel_re, kernel_im = forward(kernel_sig, jnp.zeros_like(kernel_sig), tables)
    spec_re, spec_im = forward(sig_re, sig_im, tables)
    prod_re = spec_re * kernel_re - spec_im * kernel_im
    prod_im = spec_re * kernel_im + spec_im * kernel_re
    out_re, out_im = inverse(prod_re, prod_im, tables)
    joined = jnp.stack((out_re, out_im), axis=1)
    return joined.reshape(stations, days).astype(jnp.bfloat16)


def sample_kernel(
    factor, noise, time_kernel, regions, out,
    weights, partial_weights, above, up_in, side_in, sibling, partial,
    kept, given, got, toeplitz_sum, toeplitz_diff, acc,
    up_send, up_recv, side_send, side_recv, sib_send, sib_recv, x_send, x_recv, tile_send, tile_recv,
):
    blocks = lax.axis_size("blk")
    block = lax.axis_index("blk")
    half = lax.axis_index("tm")
    core = lax.rem(block, 2)
    chip = lax.div(block, 2)
    first_chip = chip == 0
    last_chip = chip == blocks // 2 - 1
    sib = block + 1 - 2 * core
    width, local_days = noise.shape
    chunks, _, chunk = up_in.shape
    rows = width // 2
    days = acc.shape[1]

    def cols(step):
        return pl.ds(pl.multiple_of(step * chunk, chunk), chunk)

    def remote(src, dst, send, recv, where):
        return pltpu.make_async_remote_copy(
            src_ref=src, dst_ref=dst, send_sem=send, recv_sem=recv, device_id=where, device_id_type=MESH
        )

    def up_noise(step):
        return remote(noise.at[:, cols(step)], up_in.at[step], up_send.at[step], up_recv.at[step], {"blk": block + 2})

    def up_partial(step):
        return remote(partial.at[step], up_in.at[step], up_send.at[step], up_recv.at[step], {"blk": block + 2})

    def side(step):
        return remote(up_in.at[step], side_in.at[step], side_send.at[step], side_recv.at[step], {"blk": sib})

    def sib_copy(step):
        return remote(noise.at[:, cols(step)], sibling.at[step], sib_send.at[step], sib_recv.at[step], {"blk": sib})

    def cross(step):
        return remote(given.at[step], got.at[step], x_send.at[step], x_recv.at[step], {"tm": 1 - half})

    def tiles_down():
        return remote(factor.at[:, pl.ds(2 * width, 2 * width)], above, tile_send, tile_recv, {"blk": block - 2})

    barrier = pltpu.get_barrier_semaphore()
    pl.semaphore_signal(barrier, inc=1, device_id={"blk": sib}, device_id_type=MESH)
    pl.semaphore_signal(barrier, inc=1, device_id={"tm": 1 - half}, device_id_type=MESH)

    @pl.when(jnp.logical_not(first_chip))
    def _():
        pl.semaphore_signal(barrier, inc=1, device_id={"blk": block - 2}, device_id_type=MESH)

    @pl.when(jnp.logical_not(last_chip))
    def _():
        pl.semaphore_signal(barrier, inc=1, device_id={"blk": block + 2}, device_id_type=MESH)

    pl.semaphore_wait(barrier, 2 + jnp.where(first_chip, 0, 1) + jnp.where(last_chip, 0, 1))

    low = core == 0
    high = core == 1
    sends_up = jnp.logical_not(last_chip)
    takes_up = jnp.logical_not(first_chip)

    @pl.when(low & takes_up)
    def _():
        tiles_down().start()

    @pl.when(high & sends_up)
    def _():
        for step in range(AHEAD):
            up_noise(step).start()

    @pl.when(low)
    def _():
        for step in range(AHEAD):
            sib_copy(step).start()

    def valid(index, back):
        inside = index >= back
        same = regions[jnp.maximum(index - back, 0)] == regions[index]
        return jnp.where(inside & same, 1.0, 0.0).astype(jnp.float32)

    v1, v2, v3 = valid(block, 1), valid(block, 2), valid(block, 3)
    is_low = jnp.where(low, 1.0, 0.0).astype(jnp.float32)
    is_high = 1.0 - is_low
    strip = 64

    def make_weights(index, carry):
        at = pl.ds(pl.multiple_of(index * strip, strip), strip)
        row = lax.broadcasted_iota(jnp.int32, (strip, width), 0) + index * strip
        col = lax.broadcasted_iota(jnp.int32, (strip, width), 1)
        t0, t1, t2, t3 = (factor[at, pl.ds(k * width, width)].astype(jnp.float32) for k in range(4))
        eye = jnp.where(row == col, 1.0, 0.0)
        near = v1 * t1
        mid = v2 * t2
        far = v3 * t3
        first = is_low * (v3 * eye + (1.0 - v3) * mid) + is_high * mid
        second = is_low * near + is_high * far
        weights[at, pl.ds(0, width)] = jnp.where(row >= col, t0, 0.0).astype(jnp.bfloat16)
        weights[at, pl.ds(width, width)] = (is_high * near).astype(jnp.bfloat16)
        weights[at, pl.ds(2 * width, width)] = first.astype(jnp.bfloat16)
        weights[at, pl.ds(3 * width, width)] = second.astype(jnp.bfloat16)
        return carry

    lax.fori_loop(0, width // strip, make_weights, 0)

    def make_toeplitz(line, target):
        length = line.shape[1]
        wide = jnp.broadcast_to(line, (8, length))
        row_of = lax.broadcasted_iota(jnp.int32, (8, length), 0)
        base = acc.at[pl.ds(0, 8), pl.ds(0, length)]
        base[...] = wide

        def add_row(index, carry):
            base[...] = jnp.where(row_of == index, pltpu.roll(wide, index, 1), base[...])
            return carry

        lax.fori_loop(1, 8, add_row, 0)

        def add_strip(index, carry):
            upper = pltpu.roll(base[...], index * 16, 1)
            lower = pltpu.roll(base[...], index * 16 + 8, 1)
            both = jnp.concatenate([upper, lower], axis=0)
            target[pl.ds(pl.multiple_of(index * 16, 16), 16), :] = both.astype(jnp.bfloat16)
            return carry

        lax.fori_loop(0, TILE // 16, add_strip, 0)

    early, late = time_kernel[:, pl.ds(0, days // 2)], time_kernel[:, pl.ds(days // 2, days // 2)]
    make_toeplitz(0.5 * (early + late), toeplitz_sum)
    difference = 0.5 * (early - late)
    make_toeplitz(jnp.concatenate([difference, -difference], axis=1), toeplitz_diff)

    def clear(index, carry):
        acc[:, pl.ds(pl.multiple_of(index * TILE, TILE), TILE)] = jnp.zeros((rows, TILE), jnp.float32)
        return carry

    lax.fori_loop(0, days // TILE, clear, 0)

    @pl.when(low & sends_up)
    def _():
        tiles_down().wait_recv()
        uses = valid(jnp.minimum(block + 2, blocks - 1), 3)

        def make_partial_weights(index, carry):
            at = pl.ds(pl.multiple_of(index * strip, strip), strip)
            row = lax.broadcasted_iota(jnp.int32, (strip, width), 0) + index * strip
            col = lax.broadcasted_iota(jnp.int32, (strip, width), 1)
            t2, t3 = (above[at, pl.ds(k * width, width)].astype(jnp.float32) for k in range(2))
            eye = jnp.where(row == col, 1.0, 0.0)
            partial_weights[at, pl.ds(0, width)] = (uses * t2 + (1.0 - uses) * eye).astype(jnp.bfloat16)
            partial_weights[at, pl.ds(width, width)] = (uses * t3).astype(jnp.bfloat16)
            return carry

        lax.fori_loop(0, width // strip, make_partial_weights, 0)

    def dot(left, right):
        return jnp.dot(left, right, preferred_element_type=jnp.float32)

    def send_stage(step):
        nothing = jnp.zeros((width, chunk), jnp.bfloat16)

        @pl.when(high & sends_up & (step + AHEAD < chunks))
        def _():
            up_noise(step).wait_send()
            up_noise(step + AHEAD).start()

        @pl.when(low & (step + AHEAD < chunks))
        def _():
            sib_copy(step + AHEAD).start()

        @pl.when(high & takes_up)
        def _():
            up_noise(step).wait_recv()
            side(step).start()

        @pl.when(low & takes_up)
        def _():
            side(step).wait_recv()

        @pl.when(first_chip)
        def _():
            side_in[step] = nothing
            up_in[step] = nothing

        @pl.when(low)
        def _():
            sibling[step] = nothing

        @pl.when(low & sends_up)
        def _():
            for part in range(0, width, rows):
                at = pl.ds(part, rows)
                total = dot(partial_weights[at, pl.ds(0, width)], noise[:, cols(step)])
                total += dot(partial_weights[at, pl.ds(width, width)], side_in[step])
                partial[step, at, :] = total.astype(jnp.bfloat16)
            up_partial(step).start()

    def spatial(step, at):
        total = dot(weights[at, pl.ds(0, width)], noise[:, cols(step)])
        total += dot(weights[at, pl.ds(width, width)], sibling[step])
        total += dot(weights[at, pl.ds(2 * width, width)], up_in[step])
        total += dot(weights[at, pl.ds(3 * width, width)], side_in[step])
        return total.astype(jnp.bfloat16)

    def mix_stage(step):
        @pl.when(low & takes_up)
        def _():
            up_partial(step).wait_recv()
            side(step).start()

        @pl.when(high & takes_up)
        def _():
            side(step).wait_recv()

        @pl.when(high)
        def _():
            sib_copy(step).wait_recv()

        given[step] = spatial(step, pl.ds(pl.multiple_of((1 - half) * rows, rows), rows))
        cross(step).start()
        kept[step] = spatial(step, pl.ds(pl.multiple_of(half * rows, rows), rows))

    def filter_stage(step):
        cross(step).wait_recv()
        first = kept[step].astype(jnp.float32)
        second = got[step].astype(jnp.float32)
        sign = jnp.where(half == 0, 1.0, -1.0).astype(jnp.float32)
        total = (first + second).astype(jnp.bfloat16)
        difference = (sign * (first - second)).astype(jnp.bfloat16)
        start = step * chunk

        def one(index, carry):
            at = index * TILE
            sums, diffs = [], []
            for piece in range(0, chunk, TILE):
                offset = lax.rem(at - start - piece + days, days)
                folded = lax.rem(offset, days // 2)
                sums.append(toeplitz_sum[:, pl.ds(pl.multiple_of(folded, TILE), TILE)])
                diffs.append(toeplitz_diff[:, pl.ds(pl.multiple_of(offset, TILE), TILE)])
            acc[:, pl.ds(pl.multiple_of(at, TILE), TILE)] += dot(total, jnp.concatenate(sums, axis=0))
            acc[:, pl.ds(pl.multiple_of(at + days // 2, TILE), TILE)] += dot(difference, jnp.concatenate(diffs, axis=0))
            return carry

        lax.fori_loop(0, days // 2 // TILE, one, 0, unroll=4)

    def body(turn, carry):
        @pl.when(turn < chunks)
        def _():
            send_stage(turn)

        @pl.when((turn >= LEAD) & (turn < chunks + LEAD))
        def _():
            mix_stage(turn - LEAD)

        @pl.when(turn >= LEAD + 1)
        def _():
            filter_stage(turn - LEAD - 1)

        return carry

    lax.fori_loop(0, chunks + LEAD + 1, body, 0)

    def finish(index, carry):
        low_at = pl.ds(pl.multiple_of(index * TILE, TILE), TILE)
        high_at = pl.ds(pl.multiple_of(index * TILE + days // 2, TILE), TILE)
        sums, diffs = acc[:, low_at], acc[:, high_at]
        out[:, low_at] = (sums + diffs).astype(jnp.bfloat16)
        out[:, high_at] = (sums - diffs).astype(jnp.bfloat16)
        return carry

    lax.fori_loop(0, days // 2 // TILE, finish, 0)

    def drain(step, carry):
        cross(step).wait_send()

        @pl.when(takes_up)
        def _():
            side(step).wait_send()

        @pl.when(low)
        def _():
            sib_copy(step).wait_send()

        @pl.when(low & sends_up)
        def _():
            up_partial(step).wait_send()

        @pl.when(high & sends_up & (step + AHEAD >= chunks))
        def _():
            up_noise(step).wait_send()

        return carry

    lax.fori_loop(0, chunks, drain, 0)

    @pl.when(low & takes_up)
    def _():
        tiles_down().wait_send()


def fused(factor_rows, noise, time_kernel, region_of_block):
    width, local_days = noise.shape
    days = time_kernel.shape[0]
    chunks = local_days // CHUNK
    rows = width // 2
    vmem = pl.BlockSpec(memory_space=pltpu.VMEM)
    half = jnp.bfloat16
    pair = [pltpu.SemaphoreType.DMA((chunks,))] * 2
    return pl.pallas_call(
        sample_kernel,
        out_shape=jax.ShapeDtypeStruct((rows, days), half),
        in_specs=[vmem, vmem, vmem, pl.BlockSpec(memory_space=pltpu.SMEM)],
        out_specs=vmem,
        scratch_shapes=[
            pltpu.VMEM((width, 4 * width), half),
            pltpu.VMEM((width, 2 * width), half),
            pltpu.VMEM((width, 2 * width), half),
            pltpu.VMEM((chunks, width, CHUNK), half),
            pltpu.VMEM((chunks, width, CHUNK), half),
            pltpu.VMEM((chunks, width, CHUNK), half),
            pltpu.VMEM((chunks, width, CHUNK), half),
            pltpu.VMEM((chunks, rows, CHUNK), half),
            pltpu.VMEM((chunks, rows, CHUNK), half),
            pltpu.VMEM((chunks, rows, CHUNK), half),
            pltpu.VMEM((TILE, days // 2), half),
            pltpu.VMEM((TILE, days), half),
            pltpu.VMEM((rows, days), jnp.float32),
        ]
        + pair * 4
        + [pltpu.SemaphoreType.DMA, pltpu.SemaphoreType.DMA],
        compiler_params=pltpu.CompilerParams(
            collective_id=0, has_side_effects=True, vmem_limit_bytes=60 * 1024 * 1024
        ),
        cost_estimate=pl.CostEstimate(
            flops=rows * days * days + 8 * width * width * local_days,
            bytes_accessed=4 * width * local_days + 8 * width * width,
            transcendentals=0,
        ),
    )(factor_rows, noise, time_kernel.reshape(1, days), region_of_block)


def solution(mesh):
    placed = (P(("grp", "blk"), None), P(("grp", "blk"), ("tm", "rep")), P(), P("grp"))
    sizes = dict(mesh.shape)
    paired = sizes["tm"] == 2 and sizes["rep"] == 1 and sizes["blk"] % 2 == 0

    def program(factor_rows, noise, time_kernel, region_of_block):
        width, local_days = noise.shape
        fits = width == 2 * TILE and factor_rows.shape[1] == 4 * width
        fits = fits and 2 * local_days == time_kernel.shape[0] and local_days % CHUNK == 0 and local_days >= AHEAD * CHUNK
        run = fused if paired and fits else on_device
        return run(factor_rows, noise, time_kernel, region_of_block)

    return jax.shard_map(
        program,
        mesh=mesh,
        in_specs=placed,
        out_specs=P(("grp", "blk", "tm", "rep"), None),
        check_vma=False,
    )
```

```python
import math

import jax
import jax.numpy as jnp
from jax import lax
from jax.experimental import pallas as pl
from jax.experimental.pallas import tpu as pltpu
from jax.sharding import PartitionSpec as P

FIRST = 64
CHUNK = 256
TILE = 256
AHEAD = 6
LAG = 2
LEAD = 4
MESH = pl.DeviceIdType.MESH


def shifted(block, axis, distance):
    devices = range(lax.axis_size(axis))
    route = [(i - distance, i) for i in devices if i - distance in devices]
    return lax.ppermute(block, axis, route)


def make_tables(first, second):
    total = first * second
    row_a = lax.broadcasted_iota(jnp.int32, (first, first), 0)
    col_a = lax.broadcasted_iota(jnp.int32, (first, first), 1)
    angle_one = 2.0 * math.pi / first * (row_a * col_a % first).astype(jnp.float32)
    row_t = lax.broadcasted_iota(jnp.int32, (first, second), 0)
    col_t = lax.broadcasted_iota(jnp.int32, (first, second), 1)
    angle_tw = 2.0 * math.pi / total * (row_t * col_t % total).astype(jnp.float32)
    row_b = lax.broadcasted_iota(jnp.int32, (second, second), 0)
    col_b = lax.broadcasted_iota(jnp.int32, (second, second), 1)
    angle_two = 2.0 * math.pi / second * (row_b * col_b % second).astype(jnp.float32)
    return (
        jnp.cos(angle_one),
        -jnp.sin(angle_one),
        jnp.cos(angle_tw),
        -jnp.sin(angle_tw),
        jnp.cos(angle_two),
        -jnp.sin(angle_two),
    )


def left_apply(table, values):
    return jnp.einsum(
        "kn,rnm->rkm", table, values.astype(jnp.float32), precision=lax.Precision.HIGH
    )


def right_apply(values, table):
    return jnp.einsum("rkn,nm->rkm", values, table, precision=lax.Precision.HIGH)


def forward(sig_re, sig_im, tables):
    one_re, one_im, tw_re, tw_im, two_re, two_im = tables
    first_re = left_apply(one_re, sig_re) - left_apply(one_im, sig_im)
    first_im = left_apply(one_re, sig_im) + left_apply(one_im, sig_re)
    turned_re = first_re * tw_re - first_im * tw_im
    turned_im = first_re * tw_im + first_im * tw_re
    spec_re = right_apply(turned_re, two_re) - right_apply(turned_im, two_im)
    spec_im = right_apply(turned_re, two_im) + right_apply(turned_im, two_re)
    return (spec_re, spec_im)


def inverse(spec_re, spec_im, tables):
    one_re, one_im, tw_re, tw_im, two_re, two_im = tables
    back_re = right_apply(spec_re, two_re) + right_apply(spec_im, two_im)
    back_im = right_apply(spec_im, two_re) - right_apply(spec_re, two_im)
    turned_re = back_re * tw_re + back_im * tw_im
    turned_im = back_im * tw_re - back_re * tw_im
    total = one_re.shape[0] * two_re.shape[0]
    out_re = (left_apply(one_re, turned_re) + left_apply(one_im, turned_im)) / total
    out_im = (left_apply(one_re, turned_im) - left_apply(one_im, turned_re)) / total
    return (out_re, out_im)


def on_device(factor_rows, noise, time_kernel, region_of_block):
    width = noise.shape[0]
    slots = factor_rows.shape[1] // width
    position = lax.axis_index("blk")
    own_region = lax.dynamic_index_in_dim(region_of_block, position, 0, keepdims=False)
    row_ids = lax.broadcasted_iota(jnp.int32, (width, width), 0)
    col_ids = lax.broadcasted_iota(jnp.int32, (width, width), 1)
    diagonal_tile = jnp.where(
        row_ids >= col_ids, factor_rows[:, :width], jnp.zeros((width, width), jnp.bfloat16)
    )
    total = jnp.dot(diagonal_tile, noise, preferred_element_type=jnp.float32)
    previous = noise
    for step in range(1, slots):
        previous = shifted(noise, "blk", step)
        source = jnp.maximum(position - step, 0)
        source_region = lax.dynamic_index_in_dim(region_of_block, source, 0, keepdims=False)
        valid = (position >= step) & (source_region == own_region)
        tile = factor_rows[:, step * width : (step + 1) * width]
        product = jnp.dot(tile, previous, preferred_element_type=jnp.float32)
        total = total + jnp.where(valid, product, jnp.zeros_like(product))
    spatial = total.astype(jnp.bfloat16)
    regrouped = lax.all_to_all(spatial, ("tm", "rep"), split_axis=0, concat_axis=1, tiled=True)
    days = regrouped.shape[1]
    stations = regrouped.shape[0]
    second = days // FIRST
    tables = make_tables(FIRST, second)
    paired = regrouped.reshape(stations // 2, 2, FIRST, second)
    sig_re = paired[:, 0]
    sig_im = paired[:, 1]
    kernel_sig = time_kernel.reshape(1, FIRST, second)
    kernel_re, kernel_im = forward(kernel_sig, jnp.zeros_like(kernel_sig), tables)
    spec_re, spec_im = forward(sig_re, sig_im, tables)
    prod_re = spec_re * kernel_re - spec_im * kernel_im
    prod_im = spec_re * kernel_im + spec_im * kernel_re
    out_re, out_im = inverse(prod_re, prod_im, tables)
    joined = jnp.stack((out_re, out_im), axis=1)
    return joined.reshape(stations, days).astype(jnp.bfloat16)


def sample_kernel(
    factor_hbm, noise_hbm, time_kernel, regions, out,
    factor, noise, staged, weights, partial_weights, above, up_in, side_in, shared,
    kept, given, got, toeplitz_sum, toeplitz_diff, acc,
    up_send, up_recv, side_send, side_recv, sib_send, sib_recv, x_send, x_recv, out_sem, tile_send, tile_recv, factor_sem, noise_sem,
):
    blocks = lax.axis_size("blk")
    block = lax.axis_index("blk")
    half = lax.axis_index("tm")
    core = lax.rem(block, 2)
    chip = lax.div(block, 2)
    first_chip = chip == 0
    last_chip = chip == blocks // 2 - 1
    sib = block + 1 - 2 * core
    width, local_days = noise.shape
    chunks, _, chunk = up_in.shape
    rows = width // 2
    days = acc.shape[1]

    def cols(step):
        return pl.ds(pl.multiple_of(step * chunk, chunk), chunk)

    def remote(src, dst, send, recv, where):
        return pltpu.make_async_remote_copy(
            src_ref=src, dst_ref=dst, send_sem=send, recv_sem=recv, device_id=where, device_id_type=MESH
        )

    def up_noise(step):
        return remote(noise_hbm.at[:, cols(step)], up_in.at[step], up_send.at[step], up_recv.at[step], {"blk": block + 2})

    def up_partial(step):
        return remote(shared.at[step], up_in.at[step], up_send.at[step], up_recv.at[step], {"blk": block + 2})

    def side(step):
        return remote(up_in.at[step], side_in.at[step], side_send.at[step], side_recv.at[step], {"blk": sib})

    def sib_copy(step):
        return remote(noise_hbm.at[:, cols(step)], shared.at[step], sib_send.at[step], sib_recv.at[step], {"blk": sib})

    def cross(step):
        return remote(given.at[step], got.at[step], x_send.at[step], x_recv.at[step], {"tm": 1 - half})

    def tiles_down():
        return remote(factor_hbm.at[:, pl.ds(2 * width, 2 * width)], above, tile_send, tile_recv, {"blk": block - 2})

    load_factor = pltpu.make_async_copy(factor_hbm, factor, factor_sem)
    load_noise = pltpu.make_async_copy(noise_hbm, noise, noise_sem)
    load_factor.start()
    barrier = pltpu.get_barrier_semaphore()
    pl.semaphore_signal(barrier, inc=1, device_id={"blk": sib}, device_id_type=MESH)
    pl.semaphore_signal(barrier, inc=1, device_id={"tm": 1 - half}, device_id_type=MESH)

    @pl.when(jnp.logical_not(first_chip))
    def _():
        pl.semaphore_signal(barrier, inc=1, device_id={"blk": block - 2}, device_id_type=MESH)

    @pl.when(jnp.logical_not(last_chip))
    def _():
        pl.semaphore_signal(barrier, inc=1, device_id={"blk": block + 2}, device_id_type=MESH)

    pl.semaphore_wait(barrier, 2 + jnp.where(first_chip, 0, 1) + jnp.where(last_chip, 0, 1))

    low = core == 0
    high = core == 1
    sends_up = jnp.logical_not(last_chip)
    takes_up = jnp.logical_not(first_chip)

    @pl.when(low & takes_up)
    def _():
        tiles_down().start()

    @pl.when(high & sends_up)
    def _():
        for step in range(AHEAD):
            up_noise(step).start()

    @pl.when(low)
    def _():
        for step in range(AHEAD):
            sib_copy(step).start()

    load_noise.start()

    def valid(index, back):
        inside = index >= back
        same = regions[jnp.maximum(index - back, 0)] == regions[index]
        return jnp.where(inside & same, 1.0, 0.0).astype(jnp.float32)

    v1, v2, v3 = valid(block, 1), valid(block, 2), valid(block, 3)
    is_low = jnp.where(low, 1.0, 0.0).astype(jnp.float32)
    is_high = 1.0 - is_low
    strip = 64

    def make_weights(index, carry):
        at = pl.ds(pl.multiple_of(index * strip, strip), strip)
        row = lax.broadcasted_iota(jnp.int32, (strip, width), 0) + index * strip
        col = lax.broadcasted_iota(jnp.int32, (strip, width), 1)
        t0, t1, t2, t3 = (factor[at, pl.ds(k * width, width)].astype(jnp.float32) for k in range(4))
        eye = jnp.where(row == col, 1.0, 0.0)
        near = v1 * t1
        mid = v2 * t2
        far = v3 * t3
        first = is_low * (v3 * eye + (1.0 - v3) * mid) + is_high * mid
        second = is_low * near + is_high * far
        weights[at, pl.ds(0, width)] = jnp.where(row >= col, t0, 0.0).astype(jnp.bfloat16)
        weights[at, pl.ds(width, width)] = (is_high * near).astype(jnp.bfloat16)
        weights[at, pl.ds(2 * width, width)] = first.astype(jnp.bfloat16)
        weights[at, pl.ds(3 * width, width)] = second.astype(jnp.bfloat16)
        return carry

    load_factor.wait()
    lax.fori_loop(0, width // strip, make_weights, 0)

    def make_toeplitz(line, target):
        length = line.shape[1]
        wide = jnp.broadcast_to(line, (8, length))
        row_of = lax.broadcasted_iota(jnp.int32, (8, length), 0)
        base = acc.at[pl.ds(0, 8), pl.ds(0, length)]
        base[...] = wide

        def add_row(index, carry):
            base[...] = jnp.where(row_of == index, pltpu.roll(wide, index, 1), base[...])
            return carry

        lax.fori_loop(1, 8, add_row, 0)

        def add_strip(index, carry):
            upper = pltpu.roll(base[...], index * 16, 1)
            lower = pltpu.roll(base[...], index * 16 + 8, 1)
            both = jnp.concatenate([upper, lower], axis=0)
            target[pl.ds(pl.multiple_of(index * 16, 16), 16), :] = both.astype(jnp.bfloat16)
            return carry

        lax.fori_loop(0, TILE // 16, add_strip, 0)

    early, late = time_kernel[:, pl.ds(0, days // 2)], time_kernel[:, pl.ds(days // 2, days // 2)]
    make_toeplitz(0.5 * (early + late), toeplitz_sum)
    difference = 0.5 * (early - late)
    make_toeplitz(jnp.concatenate([difference, -difference], axis=1), toeplitz_diff)

    def clear(index, carry):
        acc[:, pl.ds(pl.multiple_of(index * TILE, TILE), TILE)] = jnp.zeros((rows, TILE), jnp.float32)
        return carry

    lax.fori_loop(0, days // TILE, clear, 0)

    @pl.when(low & sends_up)
    def _():
        tiles_down().wait_recv()
        uses = valid(jnp.minimum(block + 2, blocks - 1), 3)

        def make_partial_weights(index, carry):
            at = pl.ds(pl.multiple_of(index * strip, strip), strip)
            row = lax.broadcasted_iota(jnp.int32, (strip, width), 0) + index * strip
            col = lax.broadcasted_iota(jnp.int32, (strip, width), 1)
            t2, t3 = (above[at, pl.ds(k * width, width)].astype(jnp.float32) for k in range(2))
            eye = jnp.where(row == col, 1.0, 0.0)
            partial_weights[at, pl.ds(0, width)] = (uses * t2 + (1.0 - uses) * eye).astype(jnp.bfloat16)
            partial_weights[at, pl.ds(width, width)] = (uses * t3).astype(jnp.bfloat16)
            return carry

        lax.fori_loop(0, width // strip, make_partial_weights, 0)

    load_noise.wait()

    def dot(left, right):
        return jnp.dot(left, right, preferred_element_type=jnp.float32)

    def send_stage(step):
        nothing = jnp.zeros((width, chunk), jnp.bfloat16)

        @pl.when(high & sends_up & (step + AHEAD < chunks))
        def _():
            up_noise(step).wait_send()
            up_noise(step + AHEAD).start()

        @pl.when(low & (step + AHEAD < chunks))
        def _():
            sib_copy(step + AHEAD).start()

        @pl.when(high & takes_up)
        def _():
            up_noise(step).wait_recv()
            side(step).start()

        @pl.when(first_chip)
        def _():
            side_in[step] = nothing
            up_in[step] = nothing

    def partial_stage(step):
        @pl.when(low & takes_up)
        def _():
            side(step).wait_recv()

        @pl.when(low & sends_up)
        def _():
            for part in range(0, width, rows):
                at = pl.ds(part, rows)
                total = dot(partial_weights[at, pl.ds(0, width)], noise[:, cols(step)])
                total += dot(partial_weights[at, pl.ds(width, width)], side_in[step])
                shared[step, at, :] = total.astype(jnp.bfloat16)
            up_partial(step).start()

    def spatial(step, at, with_sibling):
        total = dot(weights[at, pl.ds(0, width)], noise[:, cols(step)])
        if with_sibling:
            total += dot(weights[at, pl.ds(width, width)], shared[step])
        total += dot(weights[at, pl.ds(2 * width, width)], up_in[step])
        total += dot(weights[at, pl.ds(3 * width, width)], side_in[step])
        return total.astype(jnp.bfloat16)

    def mix_stage(step):
        @pl.when(low & takes_up)
        def _():
            up_partial(step).wait_recv()
            side(step).start()

        @pl.when(high & takes_up)
        def _():
            side(step).wait_recv()

        @pl.when(high)
        def _():
            sib_copy(step).wait_recv()

        send_rows = pl.ds(pl.multiple_of((1 - half) * rows, rows), rows)
        keep_rows = pl.ds(pl.multiple_of(half * rows, rows), rows)
        for chosen, with_sibling in ((low, False), (high, True)):
            @pl.when(chosen)
            def _():
                given[step] = spatial(step, send_rows, with_sibling)
                cross(step).start()
                kept[step] = spatial(step, keep_rows, with_sibling)

    def filter_stage(step, last):
        cross(step).wait_recv()
        first = kept[step].astype(jnp.float32)
        second = got[step].astype(jnp.float32)
        sign = jnp.where(half == 0, 1.0, -1.0).astype(jnp.float32)
        total = (first + second).astype(jnp.bfloat16)
        difference = (sign * (first - second)).astype(jnp.bfloat16)
        start = step * chunk

        def one(index, carry):
            at = index * TILE
            sums, diffs = [], []
            for piece in range(0, chunk, TILE):
                offset = lax.rem(at - start - piece + days, days)
                folded = lax.rem(offset, days // 2)
                sums.append(toeplitz_sum[:, pl.ds(pl.multiple_of(folded, TILE), TILE)])
                diffs.append(toeplitz_diff[:, pl.ds(pl.multiple_of(offset, TILE), TILE)])
            low_at = pl.ds(pl.multiple_of(at, TILE), TILE)
            high_at = pl.ds(pl.multiple_of(at + days // 2, TILE), TILE)
            sum_part = acc[:, low_at] + dot(total, jnp.concatenate(sums, axis=0))
            diff_part = acc[:, high_at] + dot(difference, jnp.concatenate(diffs, axis=0))
            if last:
                staged[:, low_at] = (sum_part + diff_part).astype(jnp.bfloat16)
                staged[:, high_at] = (sum_part - diff_part).astype(jnp.bfloat16)
                pltpu.make_async_copy(staged.at[:, low_at], out.at[:, low_at], out_sem.at[2 * index]).start()
                pltpu.make_async_copy(staged.at[:, high_at], out.at[:, high_at], out_sem.at[2 * index + 1]).start()
            else:
                acc[:, low_at] = sum_part
                acc[:, high_at] = diff_part
            return carry

        lax.fori_loop(0, days // 2 // TILE, one, 0, unroll=4)

    def body(turn, carry):
        @pl.when(turn < chunks)
        def _():
            send_stage(turn)

        @pl.when((turn >= LAG) & (turn < chunks + LAG))
        def _():
            partial_stage(turn - LAG)

        @pl.when((turn >= LEAD) & (turn < chunks + LEAD))
        def _():
            mix_stage(turn - LEAD)

        @pl.when(turn >= LEAD + 1)
        def _():
            filter_stage(turn - LEAD - 1, False)

        return carry

    lax.fori_loop(0, chunks + LEAD, body, 0)
    filter_stage(chunks - 1, True)

    def drain(step, carry):
        cross(step).wait_send()

        @pl.when(takes_up)
        def _():
            side(step).wait_send()

        @pl.when(low)
        def _():
            sib_copy(step).wait_send()

        @pl.when(low & sends_up)
        def _():
            up_partial(step).wait_send()

        @pl.when(high & sends_up & (step + AHEAD >= chunks))
        def _():
            up_noise(step).wait_send()

        return carry

    lax.fori_loop(0, chunks, drain, 0)

    @pl.when(low & takes_up)
    def _():
        tiles_down().wait_send()

    for index in range(days // TILE):
        half_tiles = days // 2 // TILE
        at = pl.ds((index // 2 + index % 2 * half_tiles) * TILE, TILE)
        pltpu.make_async_copy(staged.at[:, at], out.at[:, at], out_sem.at[index]).wait()


def fused(factor_rows, noise, time_kernel, region_of_block):
    width, local_days = noise.shape
    days = time_kernel.shape[0]
    chunks = local_days // CHUNK
    rows = width // 2
    vmem = pl.BlockSpec(memory_space=pltpu.VMEM)
    hbm = pl.BlockSpec(memory_space=pl.ANY)
    half = jnp.bfloat16
    pair = [pltpu.SemaphoreType.DMA((chunks,))] * 2
    return pl.pallas_call(
        sample_kernel,
        out_shape=jax.ShapeDtypeStruct((rows, days), half),
        in_specs=[hbm, hbm, vmem, pl.BlockSpec(memory_space=pltpu.SMEM)],
        out_specs=hbm,
        scratch_shapes=[
            pltpu.VMEM((width, 4 * width), half),
            pltpu.VMEM((width, local_days), half),
            pltpu.VMEM((rows, days), half),
            pltpu.VMEM((width, 4 * width), half),
            pltpu.VMEM((width, 2 * width), half),
            pltpu.VMEM((width, 2 * width), half),
            pltpu.VMEM((chunks, width, CHUNK), half),
            pltpu.VMEM((chunks, width, CHUNK), half),
            pltpu.VMEM((chunks, width, CHUNK), half),
            pltpu.VMEM((chunks, rows, CHUNK), half),
            pltpu.VMEM((chunks, rows, CHUNK), half),
            pltpu.VMEM((chunks, rows, CHUNK), half),
            pltpu.VMEM((TILE, days // 2), half),
            pltpu.VMEM((TILE, days), half),
            pltpu.VMEM((rows, days), jnp.float32),
        ]
        + pair * 4
        + [pltpu.SemaphoreType.DMA((days // TILE,))]
        + [pltpu.SemaphoreType.DMA] * 4,
        compiler_params=pltpu.CompilerParams(
            collective_id=0, has_side_effects=True, vmem_limit_bytes=60 * 1024 * 1024
        ),
        cost_estimate=pl.CostEstimate(
            flops=rows * days * days + 8 * width * width * local_days,
            bytes_accessed=4 * width * local_days + 8 * width * width,
            transcendentals=0,
        ),
    )(factor_rows, noise, time_kernel.reshape(1, days), region_of_block)


def solution(mesh):
    placed = (P(("grp", "blk"), None), P(("grp", "blk"), ("tm", "rep")), P(), P("grp"))
    sizes = dict(mesh.shape)
    paired = sizes["tm"] == 2 and sizes["rep"] == 1 and sizes["blk"] % 2 == 0

    def program(factor_rows, noise, time_kernel, region_of_block):
        width, local_days = noise.shape
        fits = width == 2 * TILE and factor_rows.shape[1] == 4 * width
        fits = fits and 2 * local_days == time_kernel.shape[0] and local_days % CHUNK == 0 and local_days >= AHEAD * CHUNK
        run = fused if paired and fits else on_device
        return run(factor_rows, noise, time_kernel, region_of_block)

    return jax.shard_map(
        program,
        mesh=mesh,
        in_specs=placed,
        out_specs=P(("grp", "blk", "tm", "rep"), None),
        check_vma=False,
    )
```

```python
import math

import jax
import jax.numpy as jnp
from jax import lax
from jax.experimental import pallas as pl
from jax.experimental.pallas import tpu as pltpu
from jax.sharding import PartitionSpec as P

FIRST = 64
CHUNK = 256
TILE = 256
AHEAD = 6
LAG = 2
LEAD = 4
MESH = pl.DeviceIdType.MESH


def shifted(block, axis, distance):
    devices = range(lax.axis_size(axis))
    route = [(i - distance, i) for i in devices if i - distance in devices]
    return lax.ppermute(block, axis, route)


def make_tables(first, second):
    total = first * second
    row_a = lax.broadcasted_iota(jnp.int32, (first, first), 0)
    col_a = lax.broadcasted_iota(jnp.int32, (first, first), 1)
    angle_one = 2.0 * math.pi / first * (row_a * col_a % first).astype(jnp.float32)
    row_t = lax.broadcasted_iota(jnp.int32, (first, second), 0)
    col_t = lax.broadcasted_iota(jnp.int32, (first, second), 1)
    angle_tw = 2.0 * math.pi / total * (row_t * col_t % total).astype(jnp.float32)
    row_b = lax.broadcasted_iota(jnp.int32, (second, second), 0)
    col_b = lax.broadcasted_iota(jnp.int32, (second, second), 1)
    angle_two = 2.0 * math.pi / second * (row_b * col_b % second).astype(jnp.float32)
    return (
        jnp.cos(angle_one),
        -jnp.sin(angle_one),
        jnp.cos(angle_tw),
        -jnp.sin(angle_tw),
        jnp.cos(angle_two),
        -jnp.sin(angle_two),
    )


def left_apply(table, values):
    return jnp.einsum(
        "kn,rnm->rkm", table, values.astype(jnp.float32), precision=lax.Precision.HIGH
    )


def right_apply(values, table):
    return jnp.einsum("rkn,nm->rkm", values, table, precision=lax.Precision.HIGH)


def forward(sig_re, sig_im, tables):
    one_re, one_im, tw_re, tw_im, two_re, two_im = tables
    first_re = left_apply(one_re, sig_re) - left_apply(one_im, sig_im)
    first_im = left_apply(one_re, sig_im) + left_apply(one_im, sig_re)
    turned_re = first_re * tw_re - first_im * tw_im
    turned_im = first_re * tw_im + first_im * tw_re
    spec_re = right_apply(turned_re, two_re) - right_apply(turned_im, two_im)
    spec_im = right_apply(turned_re, two_im) + right_apply(turned_im, two_re)
    return (spec_re, spec_im)


def inverse(spec_re, spec_im, tables):
    one_re, one_im, tw_re, tw_im, two_re, two_im = tables
    back_re = right_apply(spec_re, two_re) + right_apply(spec_im, two_im)
    back_im = right_apply(spec_im, two_re) - right_apply(spec_re, two_im)
    turned_re = back_re * tw_re + back_im * tw_im
    turned_im = back_im * tw_re - back_re * tw_im
    total = one_re.shape[0] * two_re.shape[0]
    out_re = (left_apply(one_re, turned_re) + left_apply(one_im, turned_im)) / total
    out_im = (left_apply(one_re, turned_im) - left_apply(one_im, turned_re)) / total
    return (out_re, out_im)


def on_device(factor_rows, noise, time_kernel, region_of_block):
    width = noise.shape[0]
    slots = factor_rows.shape[1] // width
    position = lax.axis_index("blk")
    own_region = lax.dynamic_index_in_dim(region_of_block, position, 0, keepdims=False)
    row_ids = lax.broadcasted_iota(jnp.int32, (width, width), 0)
    col_ids = lax.broadcasted_iota(jnp.int32, (width, width), 1)
    diagonal_tile = jnp.where(
        row_ids >= col_ids, factor_rows[:, :width], jnp.zeros((width, width), jnp.bfloat16)
    )
    total = jnp.dot(diagonal_tile, noise, preferred_element_type=jnp.float32)
    previous = noise
    for step in range(1, slots):
        previous = shifted(noise, "blk", step)
        source = jnp.maximum(position - step, 0)
        source_region = lax.dynamic_index_in_dim(region_of_block, source, 0, keepdims=False)
        valid = (position >= step) & (source_region == own_region)
        tile = factor_rows[:, step * width : (step + 1) * width]
        product = jnp.dot(tile, previous, preferred_element_type=jnp.float32)
        total = total + jnp.where(valid, product, jnp.zeros_like(product))
    spatial = total.astype(jnp.bfloat16)
    regrouped = lax.all_to_all(spatial, ("tm", "rep"), split_axis=0, concat_axis=1, tiled=True)
    days = regrouped.shape[1]
    stations = regrouped.shape[0]
    second = days // FIRST
    tables = make_tables(FIRST, second)
    paired = regrouped.reshape(stations // 2, 2, FIRST, second)
    sig_re = paired[:, 0]
    sig_im = paired[:, 1]
    kernel_sig = time_kernel.reshape(1, FIRST, second)
    kernel_re, kernel_im = forward(kernel_sig, jnp.zeros_like(kernel_sig), tables)
    spec_re, spec_im = forward(sig_re, sig_im, tables)
    prod_re = spec_re * kernel_re - spec_im * kernel_im
    prod_im = spec_re * kernel_im + spec_im * kernel_re
    out_re, out_im = inverse(prod_re, prod_im, tables)
    joined = jnp.stack((out_re, out_im), axis=1)
    return joined.reshape(stations, days).astype(jnp.bfloat16)


def sample_kernel(
    factor_hbm, noise_hbm, time_kernel, regions, out,
    factor, noise, weights, partial_weights, above, up_in, side_in, shared,
    kept, given, got, toeplitz_sum, toeplitz_diff, acc,
    up_send, up_recv, side_send, side_recv, sib_send, sib_recv, x_send, x_recv, tile_send, tile_recv, factor_sem, noise_sem,
):
    blocks = lax.axis_size("blk")
    block = lax.axis_index("blk")
    half = lax.axis_index("tm")
    core = lax.rem(block, 2)
    chip = lax.div(block, 2)
    first_chip = chip == 0
    last_chip = chip == blocks // 2 - 1
    sib = block + 1 - 2 * core
    width, local_days = noise.shape
    chunks, _, chunk = up_in.shape
    rows = width // 2
    days = acc.shape[1]

    def cols(step):
        return pl.ds(pl.multiple_of(step * chunk, chunk), chunk)

    def remote(src, dst, send, recv, where):
        return pltpu.make_async_remote_copy(
            src_ref=src, dst_ref=dst, send_sem=send, recv_sem=recv, device_id=where, device_id_type=MESH
        )

    def up_noise(step):
        return remote(noise_hbm.at[:, cols(step)], up_in.at[step], up_send.at[step], up_recv.at[step], {"blk": block + 2})

    def up_partial(step):
        return remote(shared.at[step], up_in.at[step], up_send.at[step], up_recv.at[step], {"blk": block + 2})

    def side(step):
        return remote(up_in.at[step], side_in.at[step], side_send.at[step], side_recv.at[step], {"blk": sib})

    def sib_copy(step):
        return remote(noise_hbm.at[:, cols(step)], shared.at[step], sib_send.at[step], sib_recv.at[step], {"blk": sib})

    def cross(step):
        return remote(given.at[step], got.at[step], x_send.at[step], x_recv.at[step], {"tm": 1 - half})

    def tiles_down():
        return remote(factor_hbm.at[:, pl.ds(2 * width, 2 * width)], above, tile_send, tile_recv, {"blk": block - 2})

    load_factor = pltpu.make_async_copy(factor_hbm, factor, factor_sem)
    load_noise = pltpu.make_async_copy(noise_hbm, noise, noise_sem)
    load_factor.start()
    barrier = pltpu.get_barrier_semaphore()
    pl.semaphore_signal(barrier, inc=1, device_id={"blk": sib}, device_id_type=MESH)
    pl.semaphore_signal(barrier, inc=1, device_id={"tm": 1 - half}, device_id_type=MESH)

    @pl.when(jnp.logical_not(first_chip))
    def _():
        pl.semaphore_signal(barrier, inc=1, device_id={"blk": block - 2}, device_id_type=MESH)

    @pl.when(jnp.logical_not(last_chip))
    def _():
        pl.semaphore_signal(barrier, inc=1, device_id={"blk": block + 2}, device_id_type=MESH)

    pl.semaphore_wait(barrier, 2 + jnp.where(first_chip, 0, 1) + jnp.where(last_chip, 0, 1))

    low = core == 0
    high = core == 1
    sends_up = jnp.logical_not(last_chip)
    takes_up = jnp.logical_not(first_chip)

    @pl.when(low & takes_up)
    def _():
        tiles_down().start()

    @pl.when(high & sends_up)
    def _():
        for step in range(AHEAD):
            up_noise(step).start()

    @pl.when(low)
    def _():
        for step in range(AHEAD):
            sib_copy(step).start()

    load_noise.start()

    def valid(index, back):
        inside = index >= back
        same = regions[jnp.maximum(index - back, 0)] == regions[index]
        return jnp.where(inside & same, 1.0, 0.0).astype(jnp.float32)

    v1, v2, v3 = valid(block, 1), valid(block, 2), valid(block, 3)
    is_low = jnp.where(low, 1.0, 0.0).astype(jnp.float32)
    is_high = 1.0 - is_low
    strip = 64

    def make_weights(index, carry):
        at = pl.ds(pl.multiple_of(index * strip, strip), strip)
        row = lax.broadcasted_iota(jnp.int32, (strip, width), 0) + index * strip
        col = lax.broadcasted_iota(jnp.int32, (strip, width), 1)
        t0, t1, t2, t3 = (factor[at, pl.ds(k * width, width)].astype(jnp.float32) for k in range(4))
        eye = jnp.where(row == col, 1.0, 0.0)
        near = v1 * t1
        mid = v2 * t2
        far = v3 * t3
        first = is_low * (v3 * eye + (1.0 - v3) * mid) + is_high * mid
        second = is_low * near + is_high * far
        weights[at, pl.ds(0, width)] = jnp.where(row >= col, t0, 0.0).astype(jnp.bfloat16)
        weights[at, pl.ds(width, width)] = (is_high * near).astype(jnp.bfloat16)
        weights[at, pl.ds(2 * width, width)] = first.astype(jnp.bfloat16)
        weights[at, pl.ds(3 * width, width)] = second.astype(jnp.bfloat16)
        return carry

    load_factor.wait()
    lax.fori_loop(0, width // strip, make_weights, 0)

    def make_toeplitz(line, target):
        length = line.shape[1]
        wide = jnp.broadcast_to(line, (8, length))
        row_of = lax.broadcasted_iota(jnp.int32, (8, length), 0)
        base = acc.at[pl.ds(0, 8), pl.ds(0, length)]
        base[...] = wide

        def add_row(index, carry):
            base[...] = jnp.where(row_of == index, pltpu.roll(wide, index, 1), base[...])
            return carry

        lax.fori_loop(1, 8, add_row, 0)

        def add_strip(index, carry):
            upper = pltpu.roll(base[...], index * 16, 1)
            lower = pltpu.roll(base[...], index * 16 + 8, 1)
            both = jnp.concatenate([upper, lower], axis=0)
            target[pl.ds(pl.multiple_of(index * 16, 16), 16), :] = both.astype(jnp.bfloat16)
            return carry

        lax.fori_loop(0, TILE // 16, add_strip, 0)

    early, late = time_kernel[:, pl.ds(0, days // 2)], time_kernel[:, pl.ds(days // 2, days // 2)]
    make_toeplitz(0.5 * (early + late), toeplitz_sum)
    difference = 0.5 * (early - late)
    make_toeplitz(jnp.concatenate([difference, -difference], axis=1), toeplitz_diff)

    def clear(index, carry):
        acc[:, pl.ds(pl.multiple_of(index * TILE, TILE), TILE)] = jnp.zeros((rows, TILE), jnp.float32)
        return carry

    lax.fori_loop(0, days // TILE, clear, 0)

    @pl.when(low & sends_up)
    def _():
        tiles_down().wait_recv()
        uses = valid(jnp.minimum(block + 2, blocks - 1), 3)

        def make_partial_weights(index, carry):
            at = pl.ds(pl.multiple_of(index * strip, strip), strip)
            row = lax.broadcasted_iota(jnp.int32, (strip, width), 0) + index * strip
            col = lax.broadcasted_iota(jnp.int32, (strip, width), 1)
            t2, t3 = (above[at, pl.ds(k * width, width)].astype(jnp.float32) for k in range(2))
            eye = jnp.where(row == col, 1.0, 0.0)
            partial_weights[at, pl.ds(0, width)] = (uses * t2 + (1.0 - uses) * eye).astype(jnp.bfloat16)
            partial_weights[at, pl.ds(width, width)] = (uses * t3).astype(jnp.bfloat16)
            return carry

        lax.fori_loop(0, width // strip, make_partial_weights, 0)

    load_noise.wait()

    def dot(left, right):
        return jnp.dot(left, right, preferred_element_type=jnp.float32)

    def send_stage(step):
        nothing = jnp.zeros((width, chunk), jnp.bfloat16)

        @pl.when(high & sends_up & (step + AHEAD < chunks))
        def _():
            up_noise(step).wait_send()
            up_noise(step + AHEAD).start()

        @pl.when(low & (step + AHEAD < chunks))
        def _():
            sib_copy(step + AHEAD).start()

        @pl.when(high & takes_up)
        def _():
            up_noise(step).wait_recv()
            side(step).start()

        @pl.when(first_chip)
        def _():
            side_in[step] = nothing
            up_in[step] = nothing

    def partial_stage(step):
        @pl.when(low & takes_up)
        def _():
            side(step).wait_recv()

        @pl.when(low & sends_up)
        def _():
            for part in range(0, width, rows):
                at = pl.ds(part, rows)
                total = dot(partial_weights[at, pl.ds(0, width)], noise[:, cols(step)])
                total += dot(partial_weights[at, pl.ds(width, width)], side_in[step])
                shared[step, at, :] = total.astype(jnp.bfloat16)
            up_partial(step).start()

    def spatial(step, at, with_sibling):
        total = dot(weights[at, pl.ds(0, width)], noise[:, cols(step)])
        if with_sibling:
            total += dot(weights[at, pl.ds(width, width)], shared[step])
        total += dot(weights[at, pl.ds(2 * width, width)], up_in[step])
        total += dot(weights[at, pl.ds(3 * width, width)], side_in[step])
        return total.astype(jnp.bfloat16)

    def mix_stage(step):
        @pl.when(low & takes_up)
        def _():
            up_partial(step).wait_recv()
            side(step).start()

        @pl.when(high & takes_up)
        def _():
            side(step).wait_recv()

        @pl.when(high)
        def _():
            sib_copy(step).wait_recv()

        send_rows = pl.ds(pl.multiple_of((1 - half) * rows, rows), rows)
        keep_rows = pl.ds(pl.multiple_of(half * rows, rows), rows)
        for chosen, with_sibling in ((low, False), (high, True)):
            @pl.when(chosen)
            def _():
                given[step] = spatial(step, send_rows, with_sibling)
                cross(step).start()
                kept[step] = spatial(step, keep_rows, with_sibling)

    def filter_stage(steps, last):
        sign = jnp.where(half == 0, 1.0, -1.0).astype(jnp.float32)
        totals, differences = [], []
        for step in steps:
            cross(step).wait_recv()
            first = kept[step].astype(jnp.float32)
            second = got[step].astype(jnp.float32)
            totals.append((first + second).astype(jnp.bfloat16))
            differences.append((sign * (first - second)).astype(jnp.bfloat16))
        total = jnp.concatenate(totals, axis=1)
        difference = jnp.concatenate(differences, axis=1)

        def one(index, carry):
            at = index * TILE
            sums, diffs = [], []
            for step in steps:
                offset = lax.rem(at - step * chunk + days, days)
                folded = lax.rem(offset, days // 2)
                sums.append(toeplitz_sum[:, pl.ds(pl.multiple_of(folded, TILE), TILE)])
                diffs.append(toeplitz_diff[:, pl.ds(pl.multiple_of(offset, TILE), TILE)])
            low_at = pl.ds(pl.multiple_of(at, TILE), TILE)
            high_at = pl.ds(pl.multiple_of(at + days // 2, TILE), TILE)
            sum_part = acc[:, low_at] + dot(total, jnp.concatenate(sums, axis=0))
            diff_part = acc[:, high_at] + dot(difference, jnp.concatenate(diffs, axis=0))
            if last:
                out[:, low_at] = (sum_part + diff_part).astype(jnp.bfloat16)
                out[:, high_at] = (sum_part - diff_part).astype(jnp.bfloat16)
            else:
                acc[:, low_at] = sum_part
                acc[:, high_at] = diff_part
            return carry

        lax.fori_loop(0, days // 2 // TILE, one, 0, unroll=4)

    def body(turn, carry):
        @pl.when(turn < chunks)
        def _():
            send_stage(turn)

        @pl.when((turn >= LAG) & (turn < chunks + LAG))
        def _():
            partial_stage(turn - LAG)

        @pl.when((turn >= LEAD) & (turn < chunks + LEAD))
        def _():
            mix_stage(turn - LEAD)

        mixed = turn - LEAD

        @pl.when((mixed >= 2) & (lax.rem(mixed + chunks, 2) == 0))
        def _():
            filter_stage((mixed - 2, mixed - 1), False)

        return carry

    lax.fori_loop(0, chunks + LEAD, body, 0)
    filter_stage((chunks - 2,), False)
    filter_stage((chunks - 1,), True)

    def drain(step, carry):
        cross(step).wait_send()

        @pl.when(takes_up)
        def _():
            side(step).wait_send()

        @pl.when(low)
        def _():
            sib_copy(step).wait_send()

        @pl.when(low & sends_up)
        def _():
            up_partial(step).wait_send()

        @pl.when(high & sends_up & (step + AHEAD >= chunks))
        def _():
            up_noise(step).wait_send()

        return carry

    lax.fori_loop(0, chunks, drain, 0)

    @pl.when(low & takes_up)
    def _():
        tiles_down().wait_send()


def fused(factor_rows, noise, time_kernel, region_of_block):
    width, local_days = noise.shape
    days = time_kernel.shape[0]
    chunks = local_days // CHUNK
    rows = width // 2
    vmem = pl.BlockSpec(memory_space=pltpu.VMEM)
    hbm = pl.BlockSpec(memory_space=pl.ANY)
    half = jnp.bfloat16
    pair = [pltpu.SemaphoreType.DMA((chunks,))] * 2
    return pl.pallas_call(
        sample_kernel,
        out_shape=pltpu.VMEM((rows, days), half),
        in_specs=[hbm, hbm, vmem, pl.BlockSpec(memory_space=pltpu.SMEM)],
        out_specs=vmem,
        scratch_shapes=[
            pltpu.VMEM((width, 4 * width), half),
            pltpu.VMEM((width, local_days), half),
            pltpu.VMEM((width, 4 * width), half),
            pltpu.VMEM((width, 2 * width), half),
            pltpu.VMEM((width, 2 * width), half),
            pltpu.VMEM((chunks, width, CHUNK), half),
            pltpu.VMEM((chunks, width, CHUNK), half),
            pltpu.VMEM((chunks, width, CHUNK), half),
            pltpu.VMEM((chunks, rows, CHUNK), half),
            pltpu.VMEM((chunks, rows, CHUNK), half),
            pltpu.VMEM((chunks, rows, CHUNK), half),
            pltpu.VMEM((TILE, days // 2), half),
            pltpu.VMEM((TILE, days), half),
            pltpu.VMEM((rows, days), jnp.float32),
        ]
        + pair * 4
        + [pltpu.SemaphoreType.DMA] * 4,
        compiler_params=pltpu.CompilerParams(
            collective_id=0, has_side_effects=True, vmem_limit_bytes=48 * 1024 * 1024
        ),
        cost_estimate=pl.CostEstimate(
            flops=rows * days * days + 8 * width * width * local_days,
            bytes_accessed=4 * width * local_days + 8 * width * width,
            transcendentals=0,
        ),
    )(factor_rows, noise, time_kernel.reshape(1, days), region_of_block)


def solution(mesh):
    placed = (P(("grp", "blk"), None), P(("grp", "blk"), ("tm", "rep")), P(), P("grp"))
    sizes = dict(mesh.shape)
    paired = sizes["tm"] == 2 and sizes["rep"] == 1 and sizes["blk"] % 2 == 0

    def program(factor_rows, noise, time_kernel, region_of_block):
        width, local_days = noise.shape
        fits = width == 2 * TILE and CHUNK == TILE and factor_rows.shape[1] == 4 * width
        fits = fits and 2 * local_days == time_kernel.shape[0] and local_days % (2 * CHUNK) == 0 and local_days >= AHEAD * CHUNK
        run = fused if paired and fits else on_device
        return run(factor_rows, noise, time_kernel, region_of_block)

    return jax.shard_map(
        program,
        mesh=mesh,
        in_specs=placed,
        out_specs=P(("grp", "blk", "tm", "rep"), None),
        check_vma=False,
    )
```

```python
import math

import jax
import jax.numpy as jnp
from jax import lax
from jax.experimental import pallas as pl
from jax.experimental.pallas import tpu as pltpu
from jax.sharding import PartitionSpec as P

FIRST = 64
CHUNK = 256
TILE = 256
AHEAD = 4
PENDING = 2
LAG = 2
LEAD = 4
MESH = pl.DeviceIdType.MESH


def shifted(block, axis, distance):
    devices = range(lax.axis_size(axis))
    route = [(i - distance, i) for i in devices if i - distance in devices]
    return lax.ppermute(block, axis, route)


def make_tables(first, second):
    total = first * second
    row_a = lax.broadcasted_iota(jnp.int32, (first, first), 0)
    col_a = lax.broadcasted_iota(jnp.int32, (first, first), 1)
    angle_one = 2.0 * math.pi / first * (row_a * col_a % first).astype(jnp.float32)
    row_t = lax.broadcasted_iota(jnp.int32, (first, second), 0)
    col_t = lax.broadcasted_iota(jnp.int32, (first, second), 1)
    angle_tw = 2.0 * math.pi / total * (row_t * col_t % total).astype(jnp.float32)
    row_b = lax.broadcasted_iota(jnp.int32, (second, second), 0)
    col_b = lax.broadcasted_iota(jnp.int32, (second, second), 1)
    angle_two = 2.0 * math.pi / second * (row_b * col_b % second).astype(jnp.float32)
    return (
        jnp.cos(angle_one),
        -jnp.sin(angle_one),
        jnp.cos(angle_tw),
        -jnp.sin(angle_tw),
        jnp.cos(angle_two),
        -jnp.sin(angle_two),
    )


def left_apply(table, values):
    return jnp.einsum(
        "kn,rnm->rkm", table, values.astype(jnp.float32), precision=lax.Precision.HIGH
    )


def right_apply(values, table):
    return jnp.einsum("rkn,nm->rkm", values, table, precision=lax.Precision.HIGH)


def forward(sig_re, sig_im, tables):
    one_re, one_im, tw_re, tw_im, two_re, two_im = tables
    first_re = left_apply(one_re, sig_re) - left_apply(one_im, sig_im)
    first_im = left_apply(one_re, sig_im) + left_apply(one_im, sig_re)
    turned_re = first_re * tw_re - first_im * tw_im
    turned_im = first_re * tw_im + first_im * tw_re
    spec_re = right_apply(turned_re, two_re) - right_apply(turned_im, two_im)
    spec_im = right_apply(turned_re, two_im) + right_apply(turned_im, two_re)
    return (spec_re, spec_im)


def inverse(spec_re, spec_im, tables):
    one_re, one_im, tw_re, tw_im, two_re, two_im = tables
    back_re = right_apply(spec_re, two_re) + right_apply(spec_im, two_im)
    back_im = right_apply(spec_im, two_re) - right_apply(spec_re, two_im)
    turned_re = back_re * tw_re + back_im * tw_im
    turned_im = back_im * tw_re - back_re * tw_im
    total = one_re.shape[0] * two_re.shape[0]
    out_re = (left_apply(one_re, turned_re) + left_apply(one_im, turned_im)) / total
    out_im = (left_apply(one_re, turned_im) - left_apply(one_im, turned_re)) / total
    return (out_re, out_im)


def on_device(factor_rows, noise, time_kernel, region_of_block):
    width = noise.shape[0]
    slots = factor_rows.shape[1] // width
    position = lax.axis_index("blk")
    own_region = lax.dynamic_index_in_dim(region_of_block, position, 0, keepdims=False)
    row_ids = lax.broadcasted_iota(jnp.int32, (width, width), 0)
    col_ids = lax.broadcasted_iota(jnp.int32, (width, width), 1)
    diagonal_tile = jnp.where(
        row_ids >= col_ids, factor_rows[:, :width], jnp.zeros((width, width), jnp.bfloat16)
    )
    total = jnp.dot(diagonal_tile, noise, preferred_element_type=jnp.float32)
    previous = noise
    for step in range(1, slots):
        previous = shifted(noise, "blk", step)
        source = jnp.maximum(position - step, 0)
        source_region = lax.dynamic_index_in_dim(region_of_block, source, 0, keepdims=False)
        valid = (position >= step) & (source_region == own_region)
        tile = factor_rows[:, step * width : (step + 1) * width]
        product = jnp.dot(tile, previous, preferred_element_type=jnp.float32)
        total = total + jnp.where(valid, product, jnp.zeros_like(product))
    spatial = total.astype(jnp.bfloat16)
    regrouped = lax.all_to_all(spatial, ("tm", "rep"), split_axis=0, concat_axis=1, tiled=True)
    days = regrouped.shape[1]
    stations = regrouped.shape[0]
    second = days // FIRST
    tables = make_tables(FIRST, second)
    paired = regrouped.reshape(stations // 2, 2, FIRST, second)
    sig_re = paired[:, 0]
    sig_im = paired[:, 1]
    kernel_sig = time_kernel.reshape(1, FIRST, second)
    kernel_re, kernel_im = forward(kernel_sig, jnp.zeros_like(kernel_sig), tables)
    spec_re, spec_im = forward(sig_re, sig_im, tables)
    prod_re = spec_re * kernel_re - spec_im * kernel_im
    prod_im = spec_re * kernel_im + spec_im * kernel_re
    out_re, out_im = inverse(prod_re, prod_im, tables)
    joined = jnp.stack((out_re, out_im), axis=1)
    return joined.reshape(stations, days).astype(jnp.bfloat16)


def sample_kernel(
    factor_hbm, noise_hbm, time_kernel, regions, out,
    factor, noise, weights, partial_weights, above, up_in, side_in, shared,
    kept, given, got, toeplitz_sum, toeplitz_diff, acc,
    up_send, up_recv, side_send, side_recv, sib_send, sib_recv, x_send, x_recv, tile_send, tile_recv, factor_sem, noise_sem,
):
    blocks = lax.axis_size("blk")
    block = lax.axis_index("blk")
    half = lax.axis_index("tm")
    core = lax.rem(block, 2)
    chip = lax.div(block, 2)
    first_chip = chip == 0
    last_chip = chip == blocks // 2 - 1
    sib = block + 1 - 2 * core
    width, local_days = noise.shape
    chunks, _, chunk = up_in.shape
    rows = width // 2
    days = acc.shape[1]

    def cols(step):
        return pl.ds(pl.multiple_of(step * chunk, chunk), chunk)

    def remote(src, dst, send, recv, where):
        return pltpu.make_async_remote_copy(
            src_ref=src, dst_ref=dst, send_sem=send, recv_sem=recv, device_id=where, device_id_type=MESH
        )

    def up_noise(step):
        return remote(noise_hbm.at[:, cols(step)], up_in.at[step], up_send.at[step], up_recv.at[step], {"blk": block + 2})

    def up_partial(step):
        return remote(shared.at[step], up_in.at[step], up_send.at[step], up_recv.at[step], {"blk": block + 2})

    def side(step):
        return remote(up_in.at[step], side_in.at[step], side_send.at[step], side_recv.at[step], {"blk": sib})

    def sib_copy(step):
        return remote(noise_hbm.at[:, cols(step)], shared.at[step], sib_send.at[step], sib_recv.at[step], {"blk": sib})

    def cross(step):
        return remote(given.at[step], got.at[step], x_send.at[step], x_recv.at[step], {"tm": 1 - half})

    def tiles_down():
        return remote(factor_hbm.at[:, pl.ds(2 * width, 2 * width)], above, tile_send, tile_recv, {"blk": block - 2})

    load_factor = pltpu.make_async_copy(factor_hbm, factor, factor_sem)
    load_noise = pltpu.make_async_copy(noise_hbm, noise, noise_sem)
    load_factor.start()
    barrier = pltpu.get_barrier_semaphore()
    pl.semaphore_signal(barrier, inc=1, device_id={"blk": sib}, device_id_type=MESH)
    pl.semaphore_signal(barrier, inc=1, device_id={"tm": 1 - half}, device_id_type=MESH)

    @pl.when(jnp.logical_not(first_chip))
    def _():
        pl.semaphore_signal(barrier, inc=1, device_id={"blk": block - 2}, device_id_type=MESH)

    @pl.when(jnp.logical_not(last_chip))
    def _():
        pl.semaphore_signal(barrier, inc=1, device_id={"blk": block + 2}, device_id_type=MESH)

    pl.semaphore_wait(barrier, 2 + jnp.where(first_chip, 0, 1) + jnp.where(last_chip, 0, 1))

    low = core == 0
    high = core == 1
    sends_up = jnp.logical_not(last_chip)
    takes_up = jnp.logical_not(first_chip)

    @pl.when(low & takes_up)
    def _():
        tiles_down().start()

    @pl.when(high & sends_up)
    def _():
        for step in range(AHEAD):
            up_noise(step).start()

    @pl.when(low)
    def _():
        for step in range(AHEAD):
            sib_copy(step).start()

    load_noise.start()

    def valid(index, back):
        inside = index >= back
        same = regions[jnp.maximum(index - back, 0)] == regions[index]
        return jnp.where(inside & same, 1.0, 0.0).astype(jnp.float32)

    v1, v2, v3 = valid(block, 1), valid(block, 2), valid(block, 3)
    is_low = jnp.where(low, 1.0, 0.0).astype(jnp.float32)
    is_high = 1.0 - is_low
    strip = 64

    def make_weights(index, carry):
        at = pl.ds(pl.multiple_of(index * strip, strip), strip)
        row = lax.broadcasted_iota(jnp.int32, (strip, width), 0) + index * strip
        col = lax.broadcasted_iota(jnp.int32, (strip, width), 1)
        t0, t1, t2, t3 = (factor[at, pl.ds(k * width, width)].astype(jnp.float32) for k in range(4))
        eye = jnp.where(row == col, 1.0, 0.0)
        near = v1 * t1
        mid = v2 * t2
        far = v3 * t3
        first = is_low * (v3 * eye + (1.0 - v3) * mid) + is_high * mid
        second = is_low * near + is_high * far
        weights[at, pl.ds(0, width)] = jnp.where(row >= col, t0, 0.0).astype(jnp.bfloat16)
        weights[at, pl.ds(width, width)] = (is_high * near).astype(jnp.bfloat16)
        weights[at, pl.ds(2 * width, width)] = first.astype(jnp.bfloat16)
        weights[at, pl.ds(3 * width, width)] = second.astype(jnp.bfloat16)
        return carry

    load_factor.wait()
    lax.fori_loop(0, width // strip, make_weights, 0)

    def make_toeplitz(line, target):
        length = line.shape[1]
        wide = jnp.broadcast_to(line, (8, length))
        row_of = lax.broadcasted_iota(jnp.int32, (8, length), 0)
        base = acc.at[pl.ds(0, 8), pl.ds(0, length)]
        base[...] = wide

        def add_row(index, carry):
            base[...] = jnp.where(row_of == index, pltpu.roll(wide, index, 1), base[...])
            return carry

        lax.fori_loop(1, 8, add_row, 0)

        def add_strip(index, carry):
            upper = pltpu.roll(base[...], index * 16, 1)
            lower = pltpu.roll(base[...], index * 16 + 8, 1)
            both = jnp.concatenate([upper, lower], axis=0)
            target[pl.ds(pl.multiple_of(index * 16, 16), 16), :] = both.astype(jnp.bfloat16)
            return carry

        lax.fori_loop(0, TILE // 16, add_strip, 0)

    early, late = time_kernel[:, pl.ds(0, days // 2)], time_kernel[:, pl.ds(days // 2, days // 2)]
    make_toeplitz(0.5 * (early + late), toeplitz_sum)
    difference = 0.5 * (early - late)
    make_toeplitz(jnp.concatenate([difference, -difference], axis=1), toeplitz_diff)

    def clear(index, carry):
        acc[:, pl.ds(pl.multiple_of(index * TILE, TILE), TILE)] = jnp.zeros((rows, TILE), jnp.float32)
        return carry

    lax.fori_loop(0, days // TILE, clear, 0)

    @pl.when(low & sends_up)
    def _():
        tiles_down().wait_recv()
        uses = valid(jnp.minimum(block + 2, blocks - 1), 3)

        def make_partial_weights(index, carry):
            at = pl.ds(pl.multiple_of(index * strip, strip), strip)
            row = lax.broadcasted_iota(jnp.int32, (strip, width), 0) + index * strip
            col = lax.broadcasted_iota(jnp.int32, (strip, width), 1)
            t2, t3 = (above[at, pl.ds(k * width, width)].astype(jnp.float32) for k in range(2))
            eye = jnp.where(row == col, 1.0, 0.0)
            partial_weights[at, pl.ds(0, width)] = (uses * t2 + (1.0 - uses) * eye).astype(jnp.bfloat16)
            partial_weights[at, pl.ds(width, width)] = (uses * t3).astype(jnp.bfloat16)
            return carry

        lax.fori_loop(0, width // strip, make_partial_weights, 0)

    load_noise.wait()

    def dot(left, right):
        return jnp.dot(left, right, preferred_element_type=jnp.float32)

    def send_stage(step):
        nothing = jnp.zeros((width, chunk), jnp.bfloat16)

        @pl.when(high & sends_up & (step + AHEAD < chunks))
        def _():
            up_noise(step).wait_send()
            up_noise(step + AHEAD).start()

        @pl.when(low & (step + AHEAD < chunks))
        def _():
            sib_copy(step + AHEAD).start()

        @pl.when(high & takes_up)
        def _():
            up_noise(step).wait_recv()
            side(step).start()

        @pl.when(first_chip)
        def _():
            side_in[step] = nothing
            up_in[step] = nothing

    def partial_stage(step):
        @pl.when(low & takes_up)
        def _():
            side(step).wait_recv()

        @pl.when(low & sends_up & (step >= PENDING))
        def _():
            up_partial(step - PENDING).wait_send()

        @pl.when(low & sends_up)
        def _():
            for part in range(0, width, rows):
                at = pl.ds(part, rows)
                total = dot(partial_weights[at, pl.ds(0, width)], noise[:, cols(step)])
                total += dot(partial_weights[at, pl.ds(width, width)], side_in[step])
                shared[step, at, :] = total.astype(jnp.bfloat16)
            up_partial(step).start()

    def spatial(step, at, with_sibling):
        total = dot(weights[at, pl.ds(0, width)], noise[:, cols(step)])
        if with_sibling:
            total += dot(weights[at, pl.ds(width, width)], shared[step])
        total += dot(weights[at, pl.ds(2 * width, width)], up_in[step])
        total += dot(weights[at, pl.ds(3 * width, width)], side_in[step])
        return total.astype(jnp.bfloat16)

    def mix_stage(step):
        @pl.when(low & takes_up)
        def _():
            up_partial(step).wait_recv()
            side(step).start()

        @pl.when(high & takes_up)
        def _():
            side(step).wait_recv()

        @pl.when(high)
        def _():
            sib_copy(step).wait_recv()

        send_rows = pl.ds(pl.multiple_of((1 - half) * rows, rows), rows)
        keep_rows = pl.ds(pl.multiple_of(half * rows, rows), rows)
        for chosen, with_sibling in ((low, False), (high, True)):
            @pl.when(chosen)
            def _():
                given[step] = spatial(step, send_rows, with_sibling)
                cross(step).start()
                kept[step] = spatial(step, keep_rows, with_sibling)

    def filter_stage(steps, last):
        sign = jnp.where(half == 0, 1.0, -1.0).astype(jnp.float32)
        totals, differences = [], []
        for step in steps:
            cross(step).wait_recv()
            first = kept[step].astype(jnp.float32)
            second = got[step].astype(jnp.float32)
            totals.append((first + second).astype(jnp.bfloat16))
            differences.append((sign * (first - second)).astype(jnp.bfloat16))
        total = jnp.concatenate(totals, axis=1)
        difference = jnp.concatenate(differences, axis=1)

        def one(index, carry):
            at = index * TILE
            sums, diffs = [], []
            for step in steps:
                offset = lax.rem(at - step * chunk + days, days)
                folded = lax.rem(offset, days // 2)
                sums.append(toeplitz_sum[:, pl.ds(pl.multiple_of(folded, TILE), TILE)])
                diffs.append(toeplitz_diff[:, pl.ds(pl.multiple_of(offset, TILE), TILE)])
            low_at = pl.ds(pl.multiple_of(at, TILE), TILE)
            high_at = pl.ds(pl.multiple_of(at + days // 2, TILE), TILE)
            sum_part = acc[:, low_at] + dot(total, jnp.concatenate(sums, axis=0))
            diff_part = acc[:, high_at] + dot(difference, jnp.concatenate(diffs, axis=0))
            if last:
                out[:, low_at] = (sum_part + diff_part).astype(jnp.bfloat16)
                out[:, high_at] = (sum_part - diff_part).astype(jnp.bfloat16)
            else:
                acc[:, low_at] = sum_part
                acc[:, high_at] = diff_part
            return carry

        lax.fori_loop(0, days // 2 // TILE, one, 0, unroll=4)

    def body(turn, carry):
        @pl.when(turn < chunks)
        def _():
            send_stage(turn)

        @pl.when((turn >= LAG) & (turn < chunks + LAG))
        def _():
            partial_stage(turn - LAG)

        @pl.when((turn >= LEAD) & (turn < chunks + LEAD))
        def _():
            mix_stage(turn - LEAD)

        mixed = turn - LEAD

        @pl.when((mixed >= 2) & (lax.rem(mixed + chunks, 2) == 0))
        def _():
            filter_stage((mixed - 2, mixed - 1), False)

        return carry

    lax.fori_loop(0, chunks + LEAD, body, 0)
    filter_stage((chunks - 2,), False)
    filter_stage((chunks - 1,), True)

    def drain(step, carry):
        cross(step).wait_send()

        @pl.when(takes_up)
        def _():
            side(step).wait_send()

        @pl.when(low)
        def _():
            sib_copy(step).wait_send()

        @pl.when(low & sends_up & (step + PENDING >= chunks))
        def _():
            up_partial(step).wait_send()

        @pl.when(high & sends_up & (step + AHEAD >= chunks))
        def _():
            up_noise(step).wait_send()

        return carry

    lax.fori_loop(0, chunks, drain, 0)

    @pl.when(low & takes_up)
    def _():
        tiles_down().wait_send()


def fused(factor_rows, noise, time_kernel, region_of_block):
    width, local_days = noise.shape
    days = time_kernel.shape[0]
    chunks = local_days // CHUNK
    rows = width // 2
    vmem = pl.BlockSpec(memory_space=pltpu.VMEM)
    hbm = pl.BlockSpec(memory_space=pl.ANY)
    half = jnp.bfloat16
    pair = [pltpu.SemaphoreType.DMA((chunks,))] * 2
    return pl.pallas_call(
        sample_kernel,
        out_shape=pltpu.VMEM((rows, days), half),
        in_specs=[hbm, hbm, vmem, pl.BlockSpec(memory_space=pltpu.SMEM)],
        out_specs=vmem,
        scratch_shapes=[
            pltpu.VMEM((width, 4 * width), half),
            pltpu.VMEM((width, local_days), half),
            pltpu.VMEM((width, 4 * width), half),
            pltpu.VMEM((width, 2 * width), half),
            pltpu.VMEM((width, 2 * width), half),
            pltpu.VMEM((chunks, width, CHUNK), half),
            pltpu.VMEM((chunks, width, CHUNK), half),
            pltpu.VMEM((chunks, width, CHUNK), half),
            pltpu.VMEM((chunks, rows, CHUNK), half),
            pltpu.VMEM((chunks, rows, CHUNK), half),
            pltpu.VMEM((chunks, rows, CHUNK), half),
            pltpu.VMEM((TILE, days // 2), half),
            pltpu.VMEM((TILE, days), half),
            pltpu.VMEM((rows, days), jnp.float32),
        ]
        + pair * 4
        + [pltpu.SemaphoreType.DMA] * 4,
        compiler_params=pltpu.CompilerParams(
            collective_id=0, has_side_effects=True, vmem_limit_bytes=56 * 1024 * 1024
        ),
        cost_estimate=pl.CostEstimate(
            flops=rows * days * days + 8 * width * width * local_days,
            bytes_accessed=4 * width * local_days + 8 * width * width,
            transcendentals=0,
        ),
    )(factor_rows, noise, time_kernel.reshape(1, days), region_of_block)


def solution(mesh):
    placed = (P(("grp", "blk"), None), P(("grp", "blk"), ("tm", "rep")), P(), P("grp"))
    sizes = dict(mesh.shape)
    paired = sizes["tm"] == 2 and sizes["rep"] == 1 and sizes["blk"] % 2 == 0

    def program(factor_rows, noise, time_kernel, region_of_block):
        width, local_days = noise.shape
        fits = width == 2 * TILE and CHUNK == TILE and factor_rows.shape[1] == 4 * width
        fits = fits and 2 * local_days == time_kernel.shape[0] and local_days % (2 * CHUNK) == 0 and local_days >= AHEAD * CHUNK
        run = fused if paired and fits else on_device
        return run(factor_rows, noise, time_kernel, region_of_block)

    return jax.shard_map(
        program,
        mesh=mesh,
        in_specs=placed,
        out_specs=P(("grp", "blk", "tm", "rep"), None),
        check_vma=False,
    )
```

```python
import math

import jax
import jax.numpy as jnp
from jax import lax
from jax.experimental import pallas as pl
from jax.experimental.pallas import tpu as pltpu
from jax.sharding import PartitionSpec as P

FIRST = 64
CHUNK = 256
TILE = 256
AHEAD = 6
EXTRA = 2
PENDING = 4
LAG = 1
LEAD = 3
MESH = pl.DeviceIdType.MESH


def shifted(block, axis, distance):
    devices = range(lax.axis_size(axis))
    route = [(i - distance, i) for i in devices if i - distance in devices]
    return lax.ppermute(block, axis, route)


def make_tables(first, second):
    total = first * second
    row_a = lax.broadcasted_iota(jnp.int32, (first, first), 0)
    col_a = lax.broadcasted_iota(jnp.int32, (first, first), 1)
    angle_one = 2.0 * math.pi / first * (row_a * col_a % first).astype(jnp.float32)
    row_t = lax.broadcasted_iota(jnp.int32, (first, second), 0)
    col_t = lax.broadcasted_iota(jnp.int32, (first, second), 1)
    angle_tw = 2.0 * math.pi / total * (row_t * col_t % total).astype(jnp.float32)
    row_b = lax.broadcasted_iota(jnp.int32, (second, second), 0)
    col_b = lax.broadcasted_iota(jnp.int32, (second, second), 1)
    angle_two = 2.0 * math.pi / second * (row_b * col_b % second).astype(jnp.float32)
    return (
        jnp.cos(angle_one),
        -jnp.sin(angle_one),
        jnp.cos(angle_tw),
        -jnp.sin(angle_tw),
        jnp.cos(angle_two),
        -jnp.sin(angle_two),
    )


def left_apply(table, values):
    return jnp.einsum(
        "kn,rnm->rkm", table, values.astype(jnp.float32), precision=lax.Precision.HIGH
    )


def right_apply(values, table):
    return jnp.einsum("rkn,nm->rkm", values, table, precision=lax.Precision.HIGH)


def forward(sig_re, sig_im, tables):
    one_re, one_im, tw_re, tw_im, two_re, two_im = tables
    first_re = left_apply(one_re, sig_re) - left_apply(one_im, sig_im)
    first_im = left_apply(one_re, sig_im) + left_apply(one_im, sig_re)
    turned_re = first_re * tw_re - first_im * tw_im
    turned_im = first_re * tw_im + first_im * tw_re
    spec_re = right_apply(turned_re, two_re) - right_apply(turned_im, two_im)
    spec_im = right_apply(turned_re, two_im) + right_apply(turned_im, two_re)
    return (spec_re, spec_im)


def inverse(spec_re, spec_im, tables):
    one_re, one_im, tw_re, tw_im, two_re, two_im = tables
    back_re = right_apply(spec_re, two_re) + right_apply(spec_im, two_im)
    back_im = right_apply(spec_im, two_re) - right_apply(spec_re, two_im)
    turned_re = back_re * tw_re + back_im * tw_im
    turned_im = back_im * tw_re - back_re * tw_im
    total = one_re.shape[0] * two_re.shape[0]
    out_re = (left_apply(one_re, turned_re) + left_apply(one_im, turned_im)) / total
    out_im = (left_apply(one_re, turned_im) - left_apply(one_im, turned_re)) / total
    return (out_re, out_im)


def on_device(factor_rows, noise, time_kernel, region_of_block):
    width = noise.shape[0]
    slots = factor_rows.shape[1] // width
    position = lax.axis_index("blk")
    own_region = lax.dynamic_index_in_dim(region_of_block, position, 0, keepdims=False)
    row_ids = lax.broadcasted_iota(jnp.int32, (width, width), 0)
    col_ids = lax.broadcasted_iota(jnp.int32, (width, width), 1)
    diagonal_tile = jnp.where(
        row_ids >= col_ids, factor_rows[:, :width], jnp.zeros((width, width), jnp.bfloat16)
    )
    total = jnp.dot(diagonal_tile, noise, preferred_element_type=jnp.float32)
    previous = noise
    for step in range(1, slots):
        previous = shifted(noise, "blk", step)
        source = jnp.maximum(position - step, 0)
        source_region = lax.dynamic_index_in_dim(region_of_block, source, 0, keepdims=False)
        valid = (position >= step) & (source_region == own_region)
        tile = factor_rows[:, step * width : (step + 1) * width]
        product = jnp.dot(tile, previous, preferred_element_type=jnp.float32)
        total = total + jnp.where(valid, product, jnp.zeros_like(product))
    spatial = total.astype(jnp.bfloat16)
    regrouped = lax.all_to_all(spatial, ("tm", "rep"), split_axis=0, concat_axis=1, tiled=True)
    days = regrouped.shape[1]
    stations = regrouped.shape[0]
    second = days // FIRST
    tables = make_tables(FIRST, second)
    paired = regrouped.reshape(stations // 2, 2, FIRST, second)
    sig_re = paired[:, 0]
    sig_im = paired[:, 1]
    kernel_sig = time_kernel.reshape(1, FIRST, second)
    kernel_re, kernel_im = forward(kernel_sig, jnp.zeros_like(kernel_sig), tables)
    spec_re, spec_im = forward(sig_re, sig_im, tables)
    prod_re = spec_re * kernel_re - spec_im * kernel_im
    prod_im = spec_re * kernel_im + spec_im * kernel_re
    out_re, out_im = inverse(prod_re, prod_im, tables)
    joined = jnp.stack((out_re, out_im), axis=1)
    return joined.reshape(stations, days).astype(jnp.bfloat16)


def sample_kernel(
    factor_hbm, noise_hbm, time_kernel, regions, out,
    factor, noise, weights, partial_weights, above, up_in, side_in, shared,
    kept, given, got, toeplitz_sum, toeplitz_diff, acc,
    up_send, up_recv, side_send, side_recv, sib_send, sib_recv, x_send, x_recv, extra_send, tile_send, tile_recv, hop_send, hop_recv, far_send, far_recv, factor_sem, noise_sem,
):
    blocks = lax.axis_size("blk")
    block = lax.axis_index("blk")
    half = lax.axis_index("tm")
    core = lax.rem(block, 2)
    chip = lax.div(block, 2)
    first_chip = chip == 0
    last_chip = chip == blocks // 2 - 1
    sib = block + 1 - 2 * core
    width, local_days = noise.shape
    chunks, _, chunk = up_in.shape
    rows = width // 2
    days = acc.shape[1]

    def cols(step):
        return pl.ds(pl.multiple_of(step * chunk, chunk), chunk)

    def remote(src, dst, send, recv, where):
        return pltpu.make_async_remote_copy(
            src_ref=src, dst_ref=dst, send_sem=send, recv_sem=recv, device_id=where, device_id_type=MESH
        )

    def up_noise(step):
        return remote(noise_hbm.at[:, cols(step)], up_in.at[step], up_send.at[step], up_recv.at[step], {"blk": block + 2})

    def up_partial(step):
        return remote(shared.at[step], up_in.at[step], up_send.at[step], up_recv.at[step], {"blk": block + 2})

    def side(step):
        return remote(up_in.at[step], side_in.at[step], side_send.at[step], side_recv.at[step], {"blk": sib})

    def sib_copy(step):
        return remote(noise_hbm.at[:, cols(step)], shared.at[step], sib_send.at[step], sib_recv.at[step], {"blk": sib})

    def cross(step):
        return remote(given.at[step], got.at[step], x_send.at[step], x_recv.at[step], {"tm": 1 - half})

    def extra(index):
        step = chunks - EXTRA + index
        return remote(shared.at[step], up_in.at[step], extra_send.at[index], up_recv.at[step], {"blk": block + 3})

    near_slot, far_slot = pl.ds(0, width), pl.ds(width, width)

    def tile_down():
        source = factor_hbm.at[:, pl.ds(2 * width, width)]
        return remote(source, above.at[:, near_slot], tile_send, tile_recv, {"blk": block - 2})

    def tile_hop():
        source = factor_hbm.at[:, pl.ds(3 * width, width)]
        return remote(source, above.at[:, far_slot], hop_send, hop_recv, {"blk": sib})

    def far_down():
        return remote(above.at[:, far_slot], above.at[:, far_slot], far_send, far_recv, {"blk": block - 3})

    load_factor = pltpu.make_async_copy(factor_hbm, factor, factor_sem)
    load_noise = pltpu.make_async_copy(noise_hbm, noise, noise_sem)
    load_factor.start()
    barrier = pltpu.get_barrier_semaphore()
    pl.semaphore_signal(barrier, inc=1, device_id={"blk": sib}, device_id_type=MESH)
    pl.semaphore_signal(barrier, inc=1, device_id={"tm": 1 - half}, device_id_type=MESH)

    @pl.when(jnp.logical_not(first_chip))
    def _():
        pl.semaphore_signal(barrier, inc=1, device_id={"blk": block - 2}, device_id_type=MESH)

    @pl.when(jnp.logical_not(last_chip))
    def _():
        pl.semaphore_signal(barrier, inc=1, device_id={"blk": block + 2}, device_id_type=MESH)

    low = core == 0
    high = core == 1
    sends_up = jnp.logical_not(last_chip)
    takes_up = jnp.logical_not(first_chip)

    @pl.when(low & sends_up)
    def _():
        pl.semaphore_signal(barrier, inc=1, device_id={"blk": block + 3}, device_id_type=MESH)

    @pl.when(high & takes_up)
    def _():
        pl.semaphore_signal(barrier, inc=1, device_id={"blk": block - 3}, device_id_type=MESH)

    diagonal = jnp.where((low & sends_up) | (high & takes_up), 1, 0)
    pl.semaphore_wait(barrier, 2 + jnp.where(first_chip, 0, 1) + jnp.where(last_chip, 0, 1) + diagonal)

    @pl.when(low & takes_up)
    def _():
        tile_hop().start()
        tile_down().start()

    @pl.when(high & sends_up)
    def _():
        up_noise(0).start()
        for index in range(EXTRA):
            sib_copy(chunks - EXTRA + index).start()
        for step in range(1, AHEAD):
            up_noise(step).start()

    @pl.when(low)
    def _():
        for step in range(AHEAD):
            sib_copy(step).start()

    load_noise.start()

    @pl.when(high & takes_up)
    def _():
        tile_hop().wait_recv()
        far_down().start()

    @pl.when(low & sends_up)
    def _():
        for index in range(EXTRA):
            sib_copy(chunks - EXTRA + index).wait_recv()
            extra(index).start()

    def valid(index, back):
        inside = index >= back
        same = regions[jnp.maximum(index - back, 0)] == regions[index]
        return jnp.where(inside & same, 1.0, 0.0).astype(jnp.float32)

    v1, v2, v3 = valid(block, 1), valid(block, 2), valid(block, 3)
    is_low = jnp.where(low, 1.0, 0.0).astype(jnp.float32)
    is_high = 1.0 - is_low
    strip = 64

    def make_weights(index, carry):
        at = pl.ds(pl.multiple_of(index * strip, strip), strip)
        row = lax.broadcasted_iota(jnp.int32, (strip, width), 0) + index * strip
        col = lax.broadcasted_iota(jnp.int32, (strip, width), 1)
        t0, t1, t2, t3 = (factor[at, pl.ds(k * width, width)].astype(jnp.float32) for k in range(4))
        eye = jnp.where(row == col, 1.0, 0.0)
        near = v1 * t1
        mid = v2 * t2
        far = v3 * t3
        first = is_low * (v3 * eye + (1.0 - v3) * mid) + is_high * mid
        second = is_low * near + is_high * far
        weights[at, pl.ds(0, width)] = jnp.where(row >= col, t0, 0.0).astype(jnp.bfloat16)
        weights[at, pl.ds(width, width)] = (is_high * near).astype(jnp.bfloat16)
        weights[at, pl.ds(2 * width, width)] = first.astype(jnp.bfloat16)
        weights[at, pl.ds(3 * width, width)] = second.astype(jnp.bfloat16)
        return carry

    load_factor.wait()
    lax.fori_loop(0, width // strip, make_weights, 0)

    def make_toeplitz(line, target):
        length = line.shape[1]
        wide = jnp.broadcast_to(line, (8, length))
        row_of = lax.broadcasted_iota(jnp.int32, (8, length), 0)
        base = acc.at[pl.ds(0, 8), pl.ds(0, length)]
        base[...] = wide

        def add_row(index, carry):
            base[...] = jnp.where(row_of == index, pltpu.roll(wide, index, 1), base[...])
            return carry

        lax.fori_loop(1, 8, add_row, 0)

        def add_strip(index, carry):
            upper = pltpu.roll(base[...], index * 16, 1)
            lower = pltpu.roll(base[...], index * 16 + 8, 1)
            both = jnp.concatenate([upper, lower], axis=0)
            target[pl.ds(pl.multiple_of(index * 16, 16), 16), :] = both.astype(jnp.bfloat16)
            return carry

        lax.fori_loop(0, TILE // 16, add_strip, 0)

    early, late = time_kernel[:, pl.ds(0, days // 2)], time_kernel[:, pl.ds(days // 2, days // 2)]
    make_toeplitz(0.5 * (early + late), toeplitz_sum)
    difference = 0.5 * (early - late)
    make_toeplitz(jnp.concatenate([difference, -difference], axis=1), toeplitz_diff)

    def clear(index, carry):
        acc[:, pl.ds(pl.multiple_of(index * TILE, TILE), TILE)] = jnp.zeros((rows, TILE), jnp.float32)
        return carry

    lax.fori_loop(0, days // TILE, clear, 0)

    @pl.when(low & sends_up)
    def _():
        tile_down().wait_recv()
        far_down().wait_recv()
        uses = valid(jnp.minimum(block + 2, blocks - 1), 3)

        def make_partial_weights(index, carry):
            at = pl.ds(pl.multiple_of(index * strip, strip), strip)
            row = lax.broadcasted_iota(jnp.int32, (strip, width), 0) + index * strip
            col = lax.broadcasted_iota(jnp.int32, (strip, width), 1)
            t2, t3 = (above[at, pl.ds(k * width, width)].astype(jnp.float32) for k in range(2))
            eye = jnp.where(row == col, 1.0, 0.0)
            partial_weights[at, pl.ds(0, width)] = (uses * t2 + (1.0 - uses) * eye).astype(jnp.bfloat16)
            partial_weights[at, pl.ds(width, width)] = (uses * t3).astype(jnp.bfloat16)
            return carry

        lax.fori_loop(0, width // strip, make_partial_weights, 0)

    load_noise.wait()

    def dot(left, right):
        return jnp.dot(left, right, preferred_element_type=jnp.float32)

    def send_stage(step):
        nothing = jnp.zeros((width, chunk), jnp.bfloat16)

        @pl.when(high & sends_up & (step + AHEAD < chunks - EXTRA))
        def _():
            up_noise(step).wait_send()
            up_noise(step + AHEAD).start()

        @pl.when(low & (step + AHEAD < chunks))
        def _():
            sib_copy(step + AHEAD).start()

        @pl.when(high & takes_up)
        def _():
            up_noise(step).wait_recv()
            side(step).start()

        @pl.when(first_chip)
        def _():
            side_in[step] = nothing
            up_in[step] = nothing

    def partial_stage(step):
        @pl.when(low & takes_up)
        def _():
            side(step).wait_recv()

        for index in range(EXTRA):
            @pl.when(low & sends_up & (step == chunks - EXTRA + index))
            def _():
                extra(index).wait_send()

        @pl.when(low & sends_up & (step >= PENDING))
        def _():
            up_partial(step - PENDING).wait_send()

        @pl.when(low & sends_up)
        def _():
            for part in range(0, width, rows):
                at = pl.ds(part, rows)
                total = dot(partial_weights[at, pl.ds(0, width)], noise[:, cols(step)])
                total += dot(partial_weights[at, pl.ds(width, width)], side_in[step])
                shared[step, at, :] = total.astype(jnp.bfloat16)
            up_partial(step).start()

    def spatial(step, at, with_sibling):
        total = dot(weights[at, pl.ds(0, width)], noise[:, cols(step)])
        if with_sibling:
            total += dot(weights[at, pl.ds(width, width)], shared[step])
        total += dot(weights[at, pl.ds(2 * width, width)], up_in[step])
        total += dot(weights[at, pl.ds(3 * width, width)], side_in[step])
        return total.astype(jnp.bfloat16)

    def mix_stage(step):
        @pl.when(low & takes_up)
        def _():
            up_partial(step).wait_recv()
            side(step).start()

        @pl.when(high & takes_up)
        def _():
            side(step).wait_recv()

        @pl.when(high)
        def _():
            sib_copy(step).wait_recv()

        send_rows = pl.ds(pl.multiple_of((1 - half) * rows, rows), rows)
        keep_rows = pl.ds(pl.multiple_of(half * rows, rows), rows)
        for chosen, with_sibling in ((low, False), (high, True)):
            @pl.when(chosen)
            def _():
                given[step] = spatial(step, send_rows, with_sibling)
                cross(step).start()
                kept[step] = spatial(step, keep_rows, with_sibling)

    def filter_stage(steps, last):
        sign = jnp.where(half == 0, 1.0, -1.0).astype(jnp.float32)
        totals, differences = [], []
        for step in steps:
            cross(step).wait_recv()
            first = kept[step].astype(jnp.float32)
            second = got[step].astype(jnp.float32)
            totals.append((first + second).astype(jnp.bfloat16))
            differences.append((sign * (first - second)).astype(jnp.bfloat16))
        total = jnp.concatenate(totals, axis=1)
        difference = jnp.concatenate(differences, axis=1)

        def one(index, carry):
            at = index * TILE
            sums, diffs = [], []
            for step in steps:
                offset = lax.rem(at - step * chunk + days, days)
                folded = lax.rem(offset, days // 2)
                sums.append(toeplitz_sum[:, pl.ds(pl.multiple_of(folded, TILE), TILE)])
                diffs.append(toeplitz_diff[:, pl.ds(pl.multiple_of(offset, TILE), TILE)])
            low_at = pl.ds(pl.multiple_of(at, TILE), TILE)
            high_at = pl.ds(pl.multiple_of(at + days // 2, TILE), TILE)
            sum_part = acc[:, low_at] + dot(total, jnp.concatenate(sums, axis=0))
            diff_part = acc[:, high_at] + dot(difference, jnp.concatenate(diffs, axis=0))
            if last:
                out[:, low_at] = (sum_part + diff_part).astype(jnp.bfloat16)
                out[:, high_at] = (sum_part - diff_part).astype(jnp.bfloat16)
            else:
                acc[:, low_at] = sum_part
                acc[:, high_at] = diff_part
            return carry

        lax.fori_loop(0, days // 2 // TILE, one, 0, unroll=4)

    def body(turn, carry):
        @pl.when(turn < chunks)
        def _():
            send_stage(turn)

        @pl.when((turn >= LAG) & (turn < chunks + LAG))
        def _():
            partial_stage(turn - LAG)

        @pl.when((turn >= LEAD) & (turn < chunks + LEAD))
        def _():
            mix_stage(turn - LEAD)

        mixed = turn - LEAD

        @pl.when(mixed >= 1)
        def _():
            filter_stage((mixed - 1,), False)

        return carry

    lax.fori_loop(0, chunks + LEAD, body, 0)
    filter_stage((chunks - 1,), True)

    def drain(step, carry):
        cross(step).wait_send()

        @pl.when(takes_up)
        def _():
            side(step).wait_send()

        @pl.when(low)
        def _():
            sib_copy(step).wait_send()

        @pl.when(low & sends_up & (step + PENDING >= chunks))
        def _():
            up_partial(step).wait_send()

        @pl.when(high & sends_up & (step + AHEAD >= chunks - EXTRA) & (step < chunks - EXTRA))
        def _():
            up_noise(step).wait_send()

        return carry

    lax.fori_loop(0, chunks, drain, 0)

    @pl.when(high & sends_up)
    def _():
        for index in range(EXTRA):
            sib_copy(chunks - EXTRA + index).wait_send()

    @pl.when(low & takes_up)
    def _():
        tile_hop().wait_send()
        tile_down().wait_send()

    @pl.when(high & takes_up)
    def _():
        far_down().wait_send()


def fused(factor_rows, noise, time_kernel, region_of_block):
    width, local_days = noise.shape
    days = time_kernel.shape[0]
    chunks = local_days // CHUNK
    rows = width // 2
    vmem = pl.BlockSpec(memory_space=pltpu.VMEM)
    hbm = pl.BlockSpec(memory_space=pl.ANY)
    half = jnp.bfloat16
    pair = [pltpu.SemaphoreType.DMA((chunks,))] * 2
    return pl.pallas_call(
        sample_kernel,
        out_shape=pltpu.VMEM((rows, days), half),
        in_specs=[hbm, hbm, vmem, pl.BlockSpec(memory_space=pltpu.SMEM)],
        out_specs=vmem,
        scratch_shapes=[
            pltpu.VMEM((width, 4 * width), half),
            pltpu.VMEM((width, local_days), half),
            pltpu.VMEM((width, 4 * width), half),
            pltpu.VMEM((width, 2 * width), half),
            pltpu.VMEM((width, 2 * width), half),
            pltpu.VMEM((chunks, width, CHUNK), half),
            pltpu.VMEM((chunks, width, CHUNK), half),
            pltpu.VMEM((chunks, width, CHUNK), half),
            pltpu.VMEM((chunks, rows, CHUNK), half),
            pltpu.VMEM((chunks, rows, CHUNK), half),
            pltpu.VMEM((chunks, rows, CHUNK), half),
            pltpu.VMEM((TILE, days // 2), half),
            pltpu.VMEM((TILE, days), half),
            pltpu.VMEM((rows, days), jnp.float32),
        ]
        + pair * 4
        + [pltpu.SemaphoreType.DMA((EXTRA,))]
        + [pltpu.SemaphoreType.DMA] * 8,
        compiler_params=pltpu.CompilerParams(
            collective_id=0, has_side_effects=True, vmem_limit_bytes=56 * 1024 * 1024
        ),
        cost_estimate=pl.CostEstimate(
            flops=rows * days * days + 8 * width * width * local_days,
            bytes_accessed=4 * width * local_days + 8 * width * width,
            transcendentals=0,
        ),
    )(factor_rows, noise, time_kernel.reshape(1, days), region_of_block)


def solution(mesh):
    placed = (P(("grp", "blk"), None), P(("grp", "blk"), ("tm", "rep")), P(), P("grp"))
    sizes = dict(mesh.shape)
    paired = sizes["tm"] == 2 and sizes["rep"] == 1 and sizes["blk"] % 2 == 0

    def program(factor_rows, noise, time_kernel, region_of_block):
        width, local_days = noise.shape
        fits = width == 2 * TILE and CHUNK == TILE and factor_rows.shape[1] == 4 * width
        fits = fits and 2 * local_days == time_kernel.shape[0] and local_days % CHUNK == 0 and local_days >= (AHEAD + EXTRA) * CHUNK
        run = fused if paired and fits else on_device
        return run(factor_rows, noise, time_kernel, region_of_block)

    return jax.shard_map(
        program,
        mesh=mesh,
        in_specs=placed,
        out_specs=P(("grp", "blk", "tm", "rep"), None),
        check_vma=False,
    )
```

```python
import math

import jax
import jax.numpy as jnp
from jax import lax
from jax.experimental import pallas as pl
from jax.experimental.pallas import tpu as pltpu
from jax.sharding import PartitionSpec as P

FIRST = 64
CHUNK = 256
TILE = 256
AHEAD = 6
EXTRA = 2
PENDING = 4
LAG = 1
LEAD = 3
MESH = pl.DeviceIdType.MESH


def shifted(block, axis, distance):
    devices = range(lax.axis_size(axis))
    route = [(i - distance, i) for i in devices if i - distance in devices]
    return lax.ppermute(block, axis, route)


def make_tables(first, second):
    total = first * second
    row_a = lax.broadcasted_iota(jnp.int32, (first, first), 0)
    col_a = lax.broadcasted_iota(jnp.int32, (first, first), 1)
    angle_one = 2.0 * math.pi / first * (row_a * col_a % first).astype(jnp.float32)
    row_t = lax.broadcasted_iota(jnp.int32, (first, second), 0)
    col_t = lax.broadcasted_iota(jnp.int32, (first, second), 1)
    angle_tw = 2.0 * math.pi / total * (row_t * col_t % total).astype(jnp.float32)
    row_b = lax.broadcasted_iota(jnp.int32, (second, second), 0)
    col_b = lax.broadcasted_iota(jnp.int32, (second, second), 1)
    angle_two = 2.0 * math.pi / second * (row_b * col_b % second).astype(jnp.float32)
    return (
        jnp.cos(angle_one),
        -jnp.sin(angle_one),
        jnp.cos(angle_tw),
        -jnp.sin(angle_tw),
        jnp.cos(angle_two),
        -jnp.sin(angle_two),
    )


def left_apply(table, values):
    return jnp.einsum(
        "kn,rnm->rkm", table, values.astype(jnp.float32), precision=lax.Precision.HIGH
    )


def right_apply(values, table):
    return jnp.einsum("rkn,nm->rkm", values, table, precision=lax.Precision.HIGH)


def forward(sig_re, sig_im, tables):
    one_re, one_im, tw_re, tw_im, two_re, two_im = tables
    first_re = left_apply(one_re, sig_re) - left_apply(one_im, sig_im)
    first_im = left_apply(one_re, sig_im) + left_apply(one_im, sig_re)
    turned_re = first_re * tw_re - first_im * tw_im
    turned_im = first_re * tw_im + first_im * tw_re
    spec_re = right_apply(turned_re, two_re) - right_apply(turned_im, two_im)
    spec_im = right_apply(turned_re, two_im) + right_apply(turned_im, two_re)
    return (spec_re, spec_im)


def inverse(spec_re, spec_im, tables):
    one_re, one_im, tw_re, tw_im, two_re, two_im = tables
    back_re = right_apply(spec_re, two_re) + right_apply(spec_im, two_im)
    back_im = right_apply(spec_im, two_re) - right_apply(spec_re, two_im)
    turned_re = back_re * tw_re + back_im * tw_im
    turned_im = back_im * tw_re - back_re * tw_im
    total = one_re.shape[0] * two_re.shape[0]
    out_re = (left_apply(one_re, turned_re) + left_apply(one_im, turned_im)) / total
    out_im = (left_apply(one_re, turned_im) - left_apply(one_im, turned_re)) / total
    return (out_re, out_im)


def on_device(factor_rows, noise, time_kernel, region_of_block):
    width = noise.shape[0]
    slots = factor_rows.shape[1] // width
    position = lax.axis_index("blk")
    own_region = lax.dynamic_index_in_dim(region_of_block, position, 0, keepdims=False)
    row_ids = lax.broadcasted_iota(jnp.int32, (width, width), 0)
    col_ids = lax.broadcasted_iota(jnp.int32, (width, width), 1)
    diagonal_tile = jnp.where(
        row_ids >= col_ids, factor_rows[:, :width], jnp.zeros((width, width), jnp.bfloat16)
    )
    total = jnp.dot(diagonal_tile, noise, preferred_element_type=jnp.float32)
    previous = noise
    for step in range(1, slots):
        previous = shifted(noise, "blk", step)
        source = jnp.maximum(position - step, 0)
        source_region = lax.dynamic_index_in_dim(region_of_block, source, 0, keepdims=False)
        valid = (position >= step) & (source_region == own_region)
        tile = factor_rows[:, step * width : (step + 1) * width]
        product = jnp.dot(tile, previous, preferred_element_type=jnp.float32)
        total = total + jnp.where(valid, product, jnp.zeros_like(product))
    spatial = total.astype(jnp.bfloat16)
    regrouped = lax.all_to_all(spatial, ("tm", "rep"), split_axis=0, concat_axis=1, tiled=True)
    days = regrouped.shape[1]
    stations = regrouped.shape[0]
    second = days // FIRST
    tables = make_tables(FIRST, second)
    paired = regrouped.reshape(stations // 2, 2, FIRST, second)
    sig_re = paired[:, 0]
    sig_im = paired[:, 1]
    kernel_sig = time_kernel.reshape(1, FIRST, second)
    kernel_re, kernel_im = forward(kernel_sig, jnp.zeros_like(kernel_sig), tables)
    spec_re, spec_im = forward(sig_re, sig_im, tables)
    prod_re = spec_re * kernel_re - spec_im * kernel_im
    prod_im = spec_re * kernel_im + spec_im * kernel_re
    out_re, out_im = inverse(prod_re, prod_im, tables)
    joined = jnp.stack((out_re, out_im), axis=1)
    return joined.reshape(stations, days).astype(jnp.bfloat16)


def sample_kernel(
    factor_hbm, noise_hbm, time_kernel, regions, out,
    factor, noise, weights, partial_weights, above, up_in, side_in, shared,
    kept, given, got, toeplitz_sum, toeplitz_diff, acc,
    up_send, up_recv, side_send, side_recv, sib_send, sib_recv, x_send, x_recv, extra_send, tile_send, tile_recv, hop_send, hop_recv, far_send, far_recv, factor_sem, noise_sem,
):
    blocks = lax.axis_size("blk")
    block = lax.axis_index("blk")
    half = lax.axis_index("tm")
    core = lax.rem(block, 2)
    chip = lax.div(block, 2)
    first_chip = chip == 0
    last_chip = chip == blocks // 2 - 1
    sib = block + 1 - 2 * core
    width, local_days = noise.shape
    chunks, _, chunk = up_in.shape
    rows = width // 2
    days = acc.shape[1]

    def cols(step):
        return pl.ds(pl.multiple_of(step * chunk, chunk), chunk)

    def remote(src, dst, send, recv, where):
        return pltpu.make_async_remote_copy(
            src_ref=src, dst_ref=dst, send_sem=send, recv_sem=recv, device_id=where, device_id_type=MESH
        )

    def up_noise(step):
        return remote(noise_hbm.at[:, cols(step)], up_in.at[step], up_send.at[step], up_recv.at[step], {"blk": block + 2})

    def up_partial(step):
        return remote(shared.at[step], up_in.at[step], up_send.at[step], up_recv.at[step], {"blk": block + 2})

    def side(step):
        return remote(up_in.at[step], side_in.at[step], side_send.at[step], side_recv.at[step], {"blk": sib})

    def sib_copy(step):
        return remote(noise_hbm.at[:, cols(step)], shared.at[step], sib_send.at[step], sib_recv.at[step], {"blk": sib})

    def cross(step):
        return remote(given.at[step], got.at[step], x_send.at[step], x_recv.at[step], {"tm": 1 - half})

    def extra(index):
        step = chunks - EXTRA + index
        return remote(shared.at[step], up_in.at[step], extra_send.at[index], up_recv.at[step], {"blk": block + 3})

    near_slot, far_slot = pl.ds(0, width), pl.ds(width, width)

    def tile_down():
        source = factor_hbm.at[:, pl.ds(2 * width, width)]
        return remote(source, above.at[:, near_slot], tile_send, tile_recv, {"blk": block - 2})

    def tile_hop():
        source = factor_hbm.at[:, pl.ds(3 * width, width)]
        return remote(source, above.at[:, far_slot], hop_send, hop_recv, {"blk": sib})

    def far_down():
        return remote(above.at[:, far_slot], above.at[:, far_slot], far_send, far_recv, {"blk": block - 3})

    load_factor = pltpu.make_async_copy(factor_hbm, factor, factor_sem)
    load_noise = pltpu.make_async_copy(noise_hbm, noise, noise_sem)
    load_factor.start()
    barrier = pltpu.get_barrier_semaphore()
    pl.semaphore_signal(barrier, inc=1, device_id={"blk": sib}, device_id_type=MESH)
    pl.semaphore_signal(barrier, inc=1, device_id={"tm": 1 - half}, device_id_type=MESH)

    @pl.when(jnp.logical_not(first_chip))
    def _():
        pl.semaphore_signal(barrier, inc=1, device_id={"blk": block - 2}, device_id_type=MESH)

    @pl.when(jnp.logical_not(last_chip))
    def _():
        pl.semaphore_signal(barrier, inc=1, device_id={"blk": block + 2}, device_id_type=MESH)

    low = core == 0
    high = core == 1
    sends_up = jnp.logical_not(last_chip)
    takes_up = jnp.logical_not(first_chip)

    @pl.when(low & sends_up)
    def _():
        pl.semaphore_signal(barrier, inc=1, device_id={"blk": block + 3}, device_id_type=MESH)

    @pl.when(high & takes_up)
    def _():
        pl.semaphore_signal(barrier, inc=1, device_id={"blk": block - 3}, device_id_type=MESH)

    diagonal = jnp.where((low & sends_up) | (high & takes_up), 1, 0)
    pl.semaphore_wait(barrier, 2 + jnp.where(first_chip, 0, 1) + jnp.where(last_chip, 0, 1) + diagonal)

    @pl.when(low & takes_up)
    def _():
        tile_hop().start()
        tile_down().start()

    @pl.when(high & sends_up)
    def _():
        up_noise(0).start()
        for index in range(EXTRA):
            sib_copy(chunks - EXTRA + index).start()
        for step in range(1, AHEAD):
            up_noise(step).start()

    @pl.when(low)
    def _():
        for step in range(AHEAD):
            sib_copy(step).start()

    load_noise.start()

    @pl.when(high & takes_up)
    def _():
        tile_hop().wait_recv()
        far_down().start()

    @pl.when(low & sends_up)
    def _():
        for index in range(EXTRA):
            sib_copy(chunks - EXTRA + index).wait_recv()
            extra(index).start()

    def valid(index, back):
        inside = index >= back
        same = regions[jnp.maximum(index - back, 0)] == regions[index]
        return jnp.where(inside & same, 1.0, 0.0).astype(jnp.float32)

    v1, v2, v3 = valid(block, 1), valid(block, 2), valid(block, 3)
    is_low = jnp.where(low, 1.0, 0.0).astype(jnp.float32)
    is_high = 1.0 - is_low
    strip = 64

    def make_weights(index, carry):
        at = pl.ds(pl.multiple_of(index * strip, strip), strip)
        row = lax.broadcasted_iota(jnp.int32, (strip, width), 0) + index * strip
        col = lax.broadcasted_iota(jnp.int32, (strip, width), 1)
        t0, t1, t2, t3 = (factor[at, pl.ds(k * width, width)].astype(jnp.float32) for k in range(4))
        eye = jnp.where(row == col, 1.0, 0.0)
        near = v1 * t1
        mid = v2 * t2
        far = v3 * t3
        first = is_low * (v3 * eye + (1.0 - v3) * mid) + is_high * mid
        second = is_low * near + is_high * far
        weights[at, pl.ds(0, width)] = jnp.where(row >= col, t0, 0.0).astype(jnp.bfloat16)
        weights[at, pl.ds(width, width)] = (is_high * near).astype(jnp.bfloat16)
        weights[at, pl.ds(2 * width, width)] = first.astype(jnp.bfloat16)
        weights[at, pl.ds(3 * width, width)] = second.astype(jnp.bfloat16)
        return carry

    load_factor.wait()
    lax.fori_loop(0, width // strip, make_weights, 0)

    def make_toeplitz(line, target):
        length = line.shape[1]
        wide = jnp.broadcast_to(line, (8, length))
        row_of = lax.broadcasted_iota(jnp.int32, (8, length), 0)
        base = acc.at[pl.ds(0, 8), pl.ds(0, length)]
        base[...] = wide

        def add_row(index, carry):
            base[...] = jnp.where(row_of == index, pltpu.roll(wide, index, 1), base[...])
            return carry

        lax.fori_loop(1, 8, add_row, 0)

        def add_strip(index, carry):
            upper = pltpu.roll(base[...], index * 16, 1)
            lower = pltpu.roll(base[...], index * 16 + 8, 1)
            both = jnp.concatenate([upper, lower], axis=0)
            target[pl.ds(pl.multiple_of(index * 16, 16), 16), :] = both.astype(jnp.bfloat16)
            return carry

        lax.fori_loop(0, TILE // 16, add_strip, 0)

    def clear(index, carry):
        acc[:, pl.ds(pl.multiple_of(index * TILE, TILE), TILE)] = jnp.zeros((rows, TILE), jnp.float32)
        return carry

    def make_tables():
        early, late = time_kernel[:, pl.ds(0, days // 2)], time_kernel[:, pl.ds(days // 2, days // 2)]
        make_toeplitz(0.5 * (early + late), toeplitz_sum)
        difference = 0.5 * (early - late)
        make_toeplitz(jnp.concatenate([difference, -difference], axis=1), toeplitz_diff)
        lax.fori_loop(0, days // TILE, clear, 0)

    @pl.when(low & sends_up)
    def _():
        tile_down().wait_recv()
        far_down().wait_recv()
        uses = valid(jnp.minimum(block + 2, blocks - 1), 3)

        def make_partial_weights(index, carry):
            at = pl.ds(pl.multiple_of(index * strip, strip), strip)
            row = lax.broadcasted_iota(jnp.int32, (strip, width), 0) + index * strip
            col = lax.broadcasted_iota(jnp.int32, (strip, width), 1)
            t2, t3 = (above[at, pl.ds(k * width, width)].astype(jnp.float32) for k in range(2))
            eye = jnp.where(row == col, 1.0, 0.0)
            partial_weights[at, pl.ds(0, width)] = (uses * t2 + (1.0 - uses) * eye).astype(jnp.bfloat16)
            partial_weights[at, pl.ds(width, width)] = (uses * t3).astype(jnp.bfloat16)
            return carry

        lax.fori_loop(0, width // strip, make_partial_weights, 0)

    load_noise.wait()

    def dot(left, right):
        return jnp.dot(left, right, preferred_element_type=jnp.float32)

    def send_stage(step):
        nothing = jnp.zeros((width, chunk), jnp.bfloat16)

        @pl.when(high & sends_up & (step + AHEAD < chunks - EXTRA))
        def _():
            up_noise(step).wait_send()
            up_noise(step + AHEAD).start()

        @pl.when(low & (step + AHEAD < chunks))
        def _():
            sib_copy(step + AHEAD).start()

        @pl.when(high & takes_up)
        def _():
            up_noise(step).wait_recv()
            side(step).start()

        @pl.when(first_chip)
        def _():
            side_in[step] = nothing
            up_in[step] = nothing

    def partial_stage(step):
        @pl.when(low & takes_up)
        def _():
            side(step).wait_recv()

        for index in range(EXTRA):
            @pl.when(low & sends_up & (step == chunks - EXTRA + index))
            def _():
                extra(index).wait_send()

        @pl.when(low & sends_up & (step >= PENDING))
        def _():
            up_partial(step - PENDING).wait_send()

        @pl.when(low & sends_up)
        def _():
            for part in range(0, width, rows):
                at = pl.ds(part, rows)
                total = dot(partial_weights[at, pl.ds(0, width)], noise[:, cols(step)])
                total += dot(partial_weights[at, pl.ds(width, width)], side_in[step])
                shared[step, at, :] = total.astype(jnp.bfloat16)
            up_partial(step).start()

    def spatial(step, at, with_sibling):
        total = dot(weights[at, pl.ds(0, width)], noise[:, cols(step)])
        if with_sibling:
            total += dot(weights[at, pl.ds(width, width)], shared[step])
        total += dot(weights[at, pl.ds(2 * width, width)], up_in[step])
        total += dot(weights[at, pl.ds(3 * width, width)], side_in[step])
        return total.astype(jnp.bfloat16)

    def mix_stage(step):
        @pl.when(low & takes_up)
        def _():
            up_partial(step).wait_recv()
            side(step).start()

        @pl.when(high & takes_up)
        def _():
            side(step).wait_recv()

        @pl.when(high)
        def _():
            sib_copy(step).wait_recv()

        send_rows = pl.ds(pl.multiple_of((1 - half) * rows, rows), rows)
        keep_rows = pl.ds(pl.multiple_of(half * rows, rows), rows)
        for chosen, with_sibling in ((low, False), (high, True)):
            @pl.when(chosen)
            def _():
                given[step] = spatial(step, send_rows, with_sibling)
                cross(step).start()
                kept[step] = spatial(step, keep_rows, with_sibling)

    def filter_stage(steps, last):
        sign = jnp.where(half == 0, 1.0, -1.0).astype(jnp.float32)
        totals, differences = [], []
        for step in steps:
            cross(step).wait_recv()
            first = kept[step].astype(jnp.float32)
            second = got[step].astype(jnp.float32)
            totals.append((first + second).astype(jnp.bfloat16))
            differences.append((sign * (first - second)).astype(jnp.bfloat16))
        total = jnp.concatenate(totals, axis=1)
        difference = jnp.concatenate(differences, axis=1)

        def one(index, carry):
            at = index * TILE
            sums, diffs = [], []
            for step in steps:
                offset = lax.rem(at - step * chunk + days, days)
                folded = lax.rem(offset, days // 2)
                sums.append(toeplitz_sum[:, pl.ds(pl.multiple_of(folded, TILE), TILE)])
                diffs.append(toeplitz_diff[:, pl.ds(pl.multiple_of(offset, TILE), TILE)])
            low_at = pl.ds(pl.multiple_of(at, TILE), TILE)
            high_at = pl.ds(pl.multiple_of(at + days // 2, TILE), TILE)
            sum_part = acc[:, low_at] + dot(total, jnp.concatenate(sums, axis=0))
            diff_part = acc[:, high_at] + dot(difference, jnp.concatenate(diffs, axis=0))
            if last:
                out[:, low_at] = (sum_part + diff_part).astype(jnp.bfloat16)
                out[:, high_at] = (sum_part - diff_part).astype(jnp.bfloat16)
            else:
                acc[:, low_at] = sum_part
                acc[:, high_at] = diff_part
            return carry

        lax.fori_loop(0, days // 2 // TILE, one, 0, unroll=16)

    def body(turn, carry):
        @pl.when(turn < chunks)
        def _():
            send_stage(turn)

        @pl.when((turn >= LAG) & (turn < chunks + LAG))
        def _():
            partial_stage(turn - LAG)

        @pl.when(turn == LEAD - 1)
        def _():
            make_tables()

        @pl.when((turn >= LEAD) & (turn < chunks + LEAD))
        def _():
            mix_stage(turn - LEAD)

        mixed = turn - LEAD

        @pl.when(mixed >= 1)
        def _():
            filter_stage((mixed - 1,), False)

        return carry

    lax.fori_loop(0, chunks + LEAD, body, 0)
    filter_stage((chunks - 1,), True)

    def drain(step, carry):
        cross(step).wait_send()

        @pl.when(takes_up)
        def _():
            side(step).wait_send()

        @pl.when(low)
        def _():
            sib_copy(step).wait_send()

        @pl.when(low & sends_up & (step + PENDING >= chunks))
        def _():
            up_partial(step).wait_send()

        @pl.when(high & sends_up & (step + AHEAD >= chunks - EXTRA) & (step < chunks - EXTRA))
        def _():
            up_noise(step).wait_send()

        return carry

    lax.fori_loop(0, chunks, drain, 0)

    @pl.when(high & sends_up)
    def _():
        for index in range(EXTRA):
            sib_copy(chunks - EXTRA + index).wait_send()

    @pl.when(low & takes_up)
    def _():
        tile_hop().wait_send()
        tile_down().wait_send()

    @pl.when(high & takes_up)
    def _():
        far_down().wait_send()


def fused(factor_rows, noise, time_kernel, region_of_block):
    width, local_days = noise.shape
    days = time_kernel.shape[0]
    chunks = local_days // CHUNK
    rows = width // 2
    vmem = pl.BlockSpec(memory_space=pltpu.VMEM)
    hbm = pl.BlockSpec(memory_space=pl.ANY)
    half = jnp.bfloat16
    pair = [pltpu.SemaphoreType.DMA((chunks,))] * 2
    return pl.pallas_call(
        sample_kernel,
        out_shape=pltpu.VMEM((rows, days), half),
        in_specs=[hbm, hbm, vmem, pl.BlockSpec(memory_space=pltpu.SMEM)],
        out_specs=vmem,
        scratch_shapes=[
            pltpu.VMEM((width, 4 * width), half),
            pltpu.VMEM((width, local_days), half),
            pltpu.VMEM((width, 4 * width), half),
            pltpu.VMEM((width, 2 * width), half),
            pltpu.VMEM((width, 2 * width), half),
            pltpu.VMEM((chunks, width, CHUNK), half),
            pltpu.VMEM((chunks, width, CHUNK), half),
            pltpu.VMEM((chunks, width, CHUNK), half),
            pltpu.VMEM((chunks, rows, CHUNK), half),
            pltpu.VMEM((chunks, rows, CHUNK), half),
            pltpu.VMEM((chunks, rows, CHUNK), half),
            pltpu.VMEM((TILE, days // 2), half),
            pltpu.VMEM((TILE, days), half),
            pltpu.VMEM((rows, days), jnp.float32),
        ]
        + pair * 4
        + [pltpu.SemaphoreType.DMA((EXTRA,))]
        + [pltpu.SemaphoreType.DMA] * 8,
        compiler_params=pltpu.CompilerParams(
            collective_id=0, has_side_effects=True, vmem_limit_bytes=56 * 1024 * 1024
        ),
        cost_estimate=pl.CostEstimate(
            flops=rows * days * days + 8 * width * width * local_days,
            bytes_accessed=4 * width * local_days + 8 * width * width,
            transcendentals=0,
        ),
    )(factor_rows, noise, time_kernel.reshape(1, days), region_of_block)


def solution(mesh):
    placed = (P(("grp", "blk"), None), P(("grp", "blk"), ("tm", "rep")), P(), P("grp"))
    sizes = dict(mesh.shape)
    paired = sizes["tm"] == 2 and sizes["rep"] == 1 and sizes["blk"] % 2 == 0

    def program(factor_rows, noise, time_kernel, region_of_block):
        width, local_days = noise.shape
        fits = width == 2 * TILE and CHUNK == TILE and factor_rows.shape[1] == 4 * width
        fits = fits and 2 * local_days == time_kernel.shape[0] and local_days % CHUNK == 0 and local_days >= (AHEAD + EXTRA) * CHUNK
        run = fused if paired and fits else on_device
        return run(factor_rows, noise, time_kernel, region_of_block)

    return jax.shard_map(
        program,
        mesh=mesh,
        in_specs=placed,
        out_specs=P(("grp", "blk", "tm", "rep"), None),
        check_vma=False,
    )
```

```python
import math

import jax
import jax.numpy as jnp
from jax import lax
from jax.experimental import pallas as pl
from jax.experimental.pallas import tpu as pltpu
from jax.sharding import PartitionSpec as P

FIRST = 64
CHUNK = 256
TILE = 256
AHEAD = 6
EXTRA = 1
PENDING = 8
LAG = 1
LEAD = 3
MESH = pl.DeviceIdType.MESH


def shifted(block, axis, distance):
    devices = range(lax.axis_size(axis))
    route = [(i - distance, i) for i in devices if i - distance in devices]
    return lax.ppermute(block, axis, route)


def make_tables(first, second):
    total = first * second
    row_a = lax.broadcasted_iota(jnp.int32, (first, first), 0)
    col_a = lax.broadcasted_iota(jnp.int32, (first, first), 1)
    angle_one = 2.0 * math.pi / first * (row_a * col_a % first).astype(jnp.float32)
    row_t = lax.broadcasted_iota(jnp.int32, (first, second), 0)
    col_t = lax.broadcasted_iota(jnp.int32, (first, second), 1)
    angle_tw = 2.0 * math.pi / total * (row_t * col_t % total).astype(jnp.float32)
    row_b = lax.broadcasted_iota(jnp.int32, (second, second), 0)
    col_b = lax.broadcasted_iota(jnp.int32, (second, second), 1)
    angle_two = 2.0 * math.pi / second * (row_b * col_b % second).astype(jnp.float32)
    return (
        jnp.cos(angle_one),
        -jnp.sin(angle_one),
        jnp.cos(angle_tw),
        -jnp.sin(angle_tw),
        jnp.cos(angle_two),
        -jnp.sin(angle_two),
    )


def left_apply(table, values):
    return jnp.einsum(
        "kn,rnm->rkm", table, values.astype(jnp.float32), precision=lax.Precision.HIGH
    )


def right_apply(values, table):
    return jnp.einsum("rkn,nm->rkm", values, table, precision=lax.Precision.HIGH)


def forward(sig_re, sig_im, tables):
    one_re, one_im, tw_re, tw_im, two_re, two_im = tables
    first_re = left_apply(one_re, sig_re) - left_apply(one_im, sig_im)
    first_im = left_apply(one_re, sig_im) + left_apply(one_im, sig_re)
    turned_re = first_re * tw_re - first_im * tw_im
    turned_im = first_re * tw_im + first_im * tw_re
    spec_re = right_apply(turned_re, two_re) - right_apply(turned_im, two_im)
    spec_im = right_apply(turned_re, two_im) + right_apply(turned_im, two_re)
    return (spec_re, spec_im)


def inverse(spec_re, spec_im, tables):
    one_re, one_im, tw_re, tw_im, two_re, two_im = tables
    back_re = right_apply(spec_re, two_re) + right_apply(spec_im, two_im)
    back_im = right_apply(spec_im, two_re) - right_apply(spec_re, two_im)
    turned_re = back_re * tw_re + back_im * tw_im
    turned_im = back_im * tw_re - back_re * tw_im
    total = one_re.shape[0] * two_re.shape[0]
    out_re = (left_apply(one_re, turned_re) + left_apply(one_im, turned_im)) / total
    out_im = (left_apply(one_re, turned_im) - left_apply(one_im, turned_re)) / total
    return (out_re, out_im)


def on_device(factor_rows, noise, time_kernel, region_of_block):
    width = noise.shape[0]
    slots = factor_rows.shape[1] // width
    position = lax.axis_index("blk")
    own_region = lax.dynamic_index_in_dim(region_of_block, position, 0, keepdims=False)
    row_ids = lax.broadcasted_iota(jnp.int32, (width, width), 0)
    col_ids = lax.broadcasted_iota(jnp.int32, (width, width), 1)
    diagonal_tile = jnp.where(
        row_ids >= col_ids, factor_rows[:, :width], jnp.zeros((width, width), jnp.bfloat16)
    )
    total = jnp.dot(diagonal_tile, noise, preferred_element_type=jnp.float32)
    previous = noise
    for step in range(1, slots):
        previous = shifted(noise, "blk", step)
        source = jnp.maximum(position - step, 0)
        source_region = lax.dynamic_index_in_dim(region_of_block, source, 0, keepdims=False)
        valid = (position >= step) & (source_region == own_region)
        tile = factor_rows[:, step * width : (step + 1) * width]
        product = jnp.dot(tile, previous, preferred_element_type=jnp.float32)
        total = total + jnp.where(valid, product, jnp.zeros_like(product))
    spatial = total.astype(jnp.bfloat16)
    regrouped = lax.all_to_all(spatial, ("tm", "rep"), split_axis=0, concat_axis=1, tiled=True)
    days = regrouped.shape[1]
    stations = regrouped.shape[0]
    second = days // FIRST
    tables = make_tables(FIRST, second)
    paired = regrouped.reshape(stations // 2, 2, FIRST, second)
    sig_re = paired[:, 0]
    sig_im = paired[:, 1]
    kernel_sig = time_kernel.reshape(1, FIRST, second)
    kernel_re, kernel_im = forward(kernel_sig, jnp.zeros_like(kernel_sig), tables)
    spec_re, spec_im = forward(sig_re, sig_im, tables)
    prod_re = spec_re * kernel_re - spec_im * kernel_im
    prod_im = spec_re * kernel_im + spec_im * kernel_re
    out_re, out_im = inverse(prod_re, prod_im, tables)
    joined = jnp.stack((out_re, out_im), axis=1)
    return joined.reshape(stations, days).astype(jnp.bfloat16)


def sample_kernel(
    factor_hbm, noise_hbm, time_kernel, regions, out,
    factor, noise, weights, partial_weights, above, up_in, side_in, shared,
    kept, given, got, toeplitz_sum, toeplitz_diff, acc,
    up_send, up_recv, side_send, side_recv, sib_send, sib_recv, x_send, x_recv, extra_send, tile_send, tile_recv, hop_send, hop_recv, far_send, far_recv, factor_sem, noise_sem,
):
    blocks = lax.axis_size("blk")
    block = lax.axis_index("blk")
    half = lax.axis_index("tm")
    core = lax.rem(block, 2)
    chip = lax.div(block, 2)
    first_chip = chip == 0
    last_chip = chip == blocks // 2 - 1
    sib = block + 1 - 2 * core
    width, local_days = noise.shape
    chunks, _, chunk = up_in.shape
    rows = width // 2
    days = acc.shape[1]

    def cols(step):
        return pl.ds(pl.multiple_of(step * chunk, chunk), chunk)

    def remote(src, dst, send, recv, where):
        return pltpu.make_async_remote_copy(
            src_ref=src, dst_ref=dst, send_sem=send, recv_sem=recv, device_id=where, device_id_type=MESH
        )

    def up_noise(step):
        return remote(noise_hbm.at[:, cols(step)], up_in.at[step], up_send.at[step], up_recv.at[step], {"blk": block + 2})

    def up_partial(step):
        return remote(shared.at[step], up_in.at[step], up_send.at[step], up_recv.at[step], {"blk": block + 2})

    def side(step):
        return remote(up_in.at[step], side_in.at[step], side_send.at[step], side_recv.at[step], {"blk": sib})

    def sib_copy(step):
        return remote(noise_hbm.at[:, cols(step)], shared.at[step], sib_send.at[step], sib_recv.at[step], {"blk": sib})

    def cross(step):
        return remote(given.at[step], got.at[step], x_send.at[step], x_recv.at[step], {"tm": 1 - half})

    def extra(index):
        step = chunks - EXTRA + index
        return remote(shared.at[step], up_in.at[step], extra_send.at[index], up_recv.at[step], {"blk": block + 3})

    near_slot, far_slot = pl.ds(0, width), pl.ds(width, width)

    def tile_down():
        source = factor_hbm.at[:, pl.ds(2 * width, width)]
        return remote(source, above.at[:, near_slot], tile_send, tile_recv, {"blk": block - 2})

    def tile_hop():
        source = factor_hbm.at[:, pl.ds(3 * width, width)]
        return remote(source, above.at[:, far_slot], hop_send, hop_recv, {"blk": sib})

    def far_down():
        return remote(above.at[:, far_slot], above.at[:, far_slot], far_send, far_recv, {"blk": block - 3})

    load_factor = pltpu.make_async_copy(factor_hbm, factor, factor_sem)
    load_noise = pltpu.make_async_copy(noise_hbm, noise, noise_sem)
    load_factor.start()
    barrier = pltpu.get_barrier_semaphore()
    pl.semaphore_signal(barrier, inc=1, device_id={"blk": sib}, device_id_type=MESH)
    pl.semaphore_signal(barrier, inc=1, device_id={"tm": 1 - half}, device_id_type=MESH)

    @pl.when(jnp.logical_not(first_chip))
    def _():
        pl.semaphore_signal(barrier, inc=1, device_id={"blk": block - 2}, device_id_type=MESH)

    @pl.when(jnp.logical_not(last_chip))
    def _():
        pl.semaphore_signal(barrier, inc=1, device_id={"blk": block + 2}, device_id_type=MESH)

    low = core == 0
    high = core == 1
    sends_up = jnp.logical_not(last_chip)
    takes_up = jnp.logical_not(first_chip)

    @pl.when(low & sends_up)
    def _():
        pl.semaphore_signal(barrier, inc=1, device_id={"blk": block + 3}, device_id_type=MESH)

    @pl.when(high & takes_up)
    def _():
        pl.semaphore_signal(barrier, inc=1, device_id={"blk": block - 3}, device_id_type=MESH)

    diagonal = jnp.where((low & sends_up) | (high & takes_up), 1, 0)
    pl.semaphore_wait(barrier, 2 + jnp.where(first_chip, 0, 1) + jnp.where(last_chip, 0, 1) + diagonal)

    @pl.when(low & takes_up)
    def _():
        tile_hop().start()
        tile_down().start()

    @pl.when(high & sends_up)
    def _():
        up_noise(0).start()
        for index in range(EXTRA):
            sib_copy(chunks - EXTRA + index).start()
        for step in range(1, AHEAD):
            up_noise(step).start()

    @pl.when(low)
    def _():
        for step in range(AHEAD):
            sib_copy(step).start()

    load_noise.start()

    @pl.when(high & takes_up)
    def _():
        tile_hop().wait_recv()
        far_down().start()

    @pl.when(low & sends_up)
    def _():
        for index in range(EXTRA):
            sib_copy(chunks - EXTRA + index).wait_recv()
            extra(index).start()

    def valid(index, back):
        inside = index >= back
        same = regions[jnp.maximum(index - back, 0)] == regions[index]
        return jnp.where(inside & same, 1.0, 0.0).astype(jnp.float32)

    v1, v2, v3 = valid(block, 1), valid(block, 2), valid(block, 3)
    is_low = jnp.where(low, 1.0, 0.0).astype(jnp.float32)
    is_high = 1.0 - is_low
    strip = 64

    def make_weights(index, carry):
        at = pl.ds(pl.multiple_of(index * strip, strip), strip)
        row = lax.broadcasted_iota(jnp.int32, (strip, width), 0) + index * strip
        col = lax.broadcasted_iota(jnp.int32, (strip, width), 1)
        t0, t1, t2, t3 = (factor[at, pl.ds(k * width, width)].astype(jnp.float32) for k in range(4))
        eye = jnp.where(row == col, 1.0, 0.0)
        near = v1 * t1
        mid = v2 * t2
        far = v3 * t3
        first = is_low * (v3 * eye + (1.0 - v3) * mid) + is_high * mid
        second = is_low * near + is_high * far
        weights[at, pl.ds(0, width)] = jnp.where(row >= col, t0, 0.0).astype(jnp.bfloat16)
        weights[at, pl.ds(width, width)] = (is_high * near).astype(jnp.bfloat16)
        weights[at, pl.ds(2 * width, width)] = first.astype(jnp.bfloat16)
        weights[at, pl.ds(3 * width, width)] = second.astype(jnp.bfloat16)
        return carry

    load_factor.wait()
    lax.fori_loop(0, width // strip, make_weights, 0)

    def make_toeplitz(line, target):
        length = line.shape[1]
        wide = jnp.broadcast_to(line, (8, length))
        row_of = lax.broadcasted_iota(jnp.int32, (8, length), 0)
        base = acc.at[pl.ds(0, 8), pl.ds(0, length)]
        base[...] = wide

        def add_row(index, carry):
            base[...] = jnp.where(row_of == index, pltpu.roll(wide, index, 1), base[...])
            return carry

        lax.fori_loop(1, 8, add_row, 0)

        def add_strip(index, carry):
            upper = pltpu.roll(base[...], index * 16, 1)
            lower = pltpu.roll(base[...], index * 16 + 8, 1)
            both = jnp.concatenate([upper, lower], axis=0)
            target[pl.ds(pl.multiple_of(index * 16, 16), 16), :] = both.astype(jnp.bfloat16)
            return carry

        lax.fori_loop(0, TILE // 16, add_strip, 0)

    def clear(index, carry):
        acc[:, pl.ds(pl.multiple_of(index * TILE, TILE), TILE)] = jnp.zeros((rows, TILE), jnp.float32)
        return carry

    def make_tables():
        early, late = time_kernel[:, pl.ds(0, days // 2)], time_kernel[:, pl.ds(days // 2, days // 2)]
        make_toeplitz(0.5 * (early + late), toeplitz_sum)
        difference = 0.5 * (early - late)
        make_toeplitz(jnp.concatenate([difference, -difference], axis=1), toeplitz_diff)
        lax.fori_loop(0, days // TILE, clear, 0)

    @pl.when(low & sends_up)
    def _():
        tile_down().wait_recv()
        far_down().wait_recv()
        uses = valid(jnp.minimum(block + 2, blocks - 1), 3)

        def make_partial_weights(index, carry):
            at = pl.ds(pl.multiple_of(index * strip, strip), strip)
            row = lax.broadcasted_iota(jnp.int32, (strip, width), 0) + index * strip
            col = lax.broadcasted_iota(jnp.int32, (strip, width), 1)
            t2, t3 = (above[at, pl.ds(k * width, width)].astype(jnp.float32) for k in range(2))
            eye = jnp.where(row == col, 1.0, 0.0)
            partial_weights[at, pl.ds(0, width)] = (uses * t2 + (1.0 - uses) * eye).astype(jnp.bfloat16)
            partial_weights[at, pl.ds(width, width)] = (uses * t3).astype(jnp.bfloat16)
            return carry

        lax.fori_loop(0, width // strip, make_partial_weights, 0)

    load_noise.wait()

    def dot(left, right):
        return jnp.dot(left, right, preferred_element_type=jnp.float32)

    def send_stage(step):
        nothing = jnp.zeros((width, chunk), jnp.bfloat16)

        @pl.when(high & sends_up & (step + AHEAD < chunks - EXTRA))
        def _():
            up_noise(step).wait_send()
            up_noise(step + AHEAD).start()

        @pl.when(low & (step + AHEAD < chunks))
        def _():
            sib_copy(step + AHEAD).start()

        @pl.when(high & takes_up)
        def _():
            up_noise(step).wait_recv()
            side(step).start()

        @pl.when(first_chip)
        def _():
            side_in[step] = nothing
            up_in[step] = nothing

    def partial_stage(step):
        @pl.when(low & takes_up)
        def _():
            side(step).wait_recv()

        for index in range(EXTRA):
            @pl.when(low & sends_up & (step == chunks - EXTRA + index))
            def _():
                extra(index).wait_send()

        @pl.when(low & sends_up & (step >= PENDING))
        def _():
            up_partial(step - PENDING).wait_send()

        @pl.when(low & sends_up)
        def _():
            for part in range(0, width, rows):
                at = pl.ds(part, rows)
                total = dot(partial_weights[at, pl.ds(0, width)], noise[:, cols(step)])
                total += dot(partial_weights[at, pl.ds(width, width)], side_in[step])
                shared[step, at, :] = total.astype(jnp.bfloat16)
            up_partial(step).start()

    def spatial(step, at, with_sibling):
        total = dot(weights[at, pl.ds(0, width)], noise[:, cols(step)])
        if with_sibling:
            total += dot(weights[at, pl.ds(width, width)], shared[step])
        total += dot(weights[at, pl.ds(2 * width, width)], up_in[step])
        total += dot(weights[at, pl.ds(3 * width, width)], side_in[step])
        return total.astype(jnp.bfloat16)

    def mix_stage(step):
        @pl.when(low & takes_up)
        def _():
            up_partial(step).wait_recv()
            side(step).start()

        @pl.when(high & takes_up)
        def _():
            side(step).wait_recv()

        @pl.when(high)
        def _():
            sib_copy(step).wait_recv()

        send_rows = pl.ds(pl.multiple_of((1 - half) * rows, rows), rows)
        keep_rows = pl.ds(pl.multiple_of(half * rows, rows), rows)
        for chosen, with_sibling in ((low, False), (high, True)):
            @pl.when(chosen)
            def _():
                given[step] = spatial(step, send_rows, with_sibling)
                cross(step).start()
                kept[step] = spatial(step, keep_rows, with_sibling)

    def filter_stage(steps, last):
        sign = jnp.where(half == 0, 1.0, -1.0).astype(jnp.float32)
        totals, differences = [], []
        for step in steps:
            cross(step).wait_recv()
            first = kept[step].astype(jnp.float32)
            second = got[step].astype(jnp.float32)
            totals.append((first + second).astype(jnp.bfloat16))
            differences.append((sign * (first - second)).astype(jnp.bfloat16))
        total = jnp.concatenate(totals, axis=1)
        difference = jnp.concatenate(differences, axis=1)

        def one(index, carry):
            at = index * TILE
            sums, diffs = [], []
            for step in steps:
                offset = lax.rem(at - step * chunk + days, days)
                folded = lax.rem(offset, days // 2)
                sums.append(toeplitz_sum[:, pl.ds(pl.multiple_of(folded, TILE), TILE)])
                diffs.append(toeplitz_diff[:, pl.ds(pl.multiple_of(offset, TILE), TILE)])
            low_at = pl.ds(pl.multiple_of(at, TILE), TILE)
            high_at = pl.ds(pl.multiple_of(at + days // 2, TILE), TILE)
            sum_part = acc[:, low_at] + dot(total, jnp.concatenate(sums, axis=0))
            diff_part = acc[:, high_at] + dot(difference, jnp.concatenate(diffs, axis=0))
            if last:
                out[:, low_at] = (sum_part + diff_part).astype(jnp.bfloat16)
                out[:, high_at] = (sum_part - diff_part).astype(jnp.bfloat16)
            else:
                acc[:, low_at] = sum_part
                acc[:, high_at] = diff_part
            return carry

        lax.fori_loop(0, days // 2 // TILE, one, 0, unroll=16)

    def body(turn, carry):
        @pl.when(turn < chunks)
        def _():
            send_stage(turn)

        @pl.when((turn >= LAG) & (turn < chunks + LAG))
        def _():
            partial_stage(turn - LAG)

        @pl.when(turn == LEAD - 1)
        def _():
            make_tables()

        @pl.when((turn >= LEAD) & (turn < chunks + LEAD))
        def _():
            mix_stage(turn - LEAD)

        mixed = turn - LEAD

        @pl.when(mixed >= 1)
        def _():
            filter_stage((mixed - 1,), False)

        return carry

    lax.fori_loop(0, chunks + LEAD, body, 0)
    filter_stage((chunks - 1,), True)

    def drain(step, carry):
        cross(step).wait_send()

        @pl.when(takes_up)
        def _():
            side(step).wait_send()

        @pl.when(low)
        def _():
            sib_copy(step).wait_send()

        @pl.when(low & sends_up & (step + PENDING >= chunks))
        def _():
            up_partial(step).wait_send()

        @pl.when(high & sends_up & (step + AHEAD >= chunks - EXTRA) & (step < chunks - EXTRA))
        def _():
            up_noise(step).wait_send()

        return carry

    lax.fori_loop(0, chunks, drain, 0)

    @pl.when(high & sends_up)
    def _():
        for index in range(EXTRA):
            sib_copy(chunks - EXTRA + index).wait_send()

    @pl.when(low & takes_up)
    def _():
        tile_hop().wait_send()
        tile_down().wait_send()

    @pl.when(high & takes_up)
    def _():
        far_down().wait_send()


def fused(factor_rows, noise, time_kernel, region_of_block):
    width, local_days = noise.shape
    days = time_kernel.shape[0]
    chunks = local_days // CHUNK
    rows = width // 2
    vmem = pl.BlockSpec(memory_space=pltpu.VMEM)
    hbm = pl.BlockSpec(memory_space=pl.ANY)
    half = jnp.bfloat16
    pair = [pltpu.SemaphoreType.DMA((chunks,))] * 2
    return pl.pallas_call(
        sample_kernel,
        out_shape=pltpu.VMEM((rows, days), half),
        in_specs=[hbm, hbm, vmem, pl.BlockSpec(memory_space=pltpu.SMEM)],
        out_specs=vmem,
        scratch_shapes=[
            pltpu.VMEM((width, 4 * width), half),
            pltpu.VMEM((width, local_days), half),
            pltpu.VMEM((width, 4 * width), half),
            pltpu.VMEM((width, 2 * width), half),
            pltpu.VMEM((width, 2 * width), half),
            pltpu.VMEM((chunks, width, CHUNK), half),
            pltpu.VMEM((chunks, width, CHUNK), half),
            pltpu.VMEM((chunks, width, CHUNK), half),
            pltpu.VMEM((chunks, rows, CHUNK), half),
            pltpu.VMEM((chunks, rows, CHUNK), half),
            pltpu.VMEM((chunks, rows, CHUNK), half),
            pltpu.VMEM((TILE, days // 2), half),
            pltpu.VMEM((TILE, days), half),
            pltpu.VMEM((rows, days), jnp.float32),
        ]
        + pair * 4
        + [pltpu.SemaphoreType.DMA((EXTRA,))]
        + [pltpu.SemaphoreType.DMA] * 8,
        compiler_params=pltpu.CompilerParams(
            collective_id=0, has_side_effects=True, vmem_limit_bytes=56 * 1024 * 1024
        ),
        cost_estimate=pl.CostEstimate(
            flops=rows * days * days + 8 * width * width * local_days,
            bytes_accessed=4 * width * local_days + 8 * width * width,
            transcendentals=0,
        ),
    )(factor_rows, noise, time_kernel.reshape(1, days), region_of_block)


def solution(mesh):
    placed = (P(("grp", "blk"), None), P(("grp", "blk"), ("tm", "rep")), P(), P("grp"))
    sizes = dict(mesh.shape)
    paired = sizes["tm"] == 2 and sizes["rep"] == 1 and sizes["blk"] % 2 == 0

    def program(factor_rows, noise, time_kernel, region_of_block):
        width, local_days = noise.shape
        fits = width == 2 * TILE and CHUNK == TILE and factor_rows.shape[1] == 4 * width
        fits = fits and 2 * local_days == time_kernel.shape[0] and local_days % CHUNK == 0 and local_days >= (AHEAD + EXTRA) * CHUNK
        run = fused if paired and fits else on_device
        return run(factor_rows, noise, time_kernel, region_of_block)

    return jax.shard_map(
        program,
        mesh=mesh,
        in_specs=placed,
        out_specs=P(("grp", "blk", "tm", "rep"), None),
        check_vma=False,
    )
```
